32 devices in a mesh: gx: 4 (over x, core), yz: 8 (over z, y).
Axes of the slice: x: 2, y: 2, z: 4, core: 2. Of those that a mesh axis runs over, the one named last changes fastest.
Arguments:
- displacement: float32 [3, 32, 128, 2048], P(None, 'gx', 'yz'), may hold values from -1.2 to 1.2
- force: float32 [3, 32, 128, 2048], P(None, 'gx', 'yz'), may hold values from -1.2 to 1.2
- damage: float32 [32, 128, 2048], P('gx', 'yz'), may hold values from 0 to 0.6
- history_old: float32 [32, 128, 2048], P('gx', 'yz'), may hold values from 0 to 0.5
- material: int32 [32, 128, 2048], P('gx', 'yz'), may hold values from 0 to 3
- patch_ids: int32 [32, 12], P(('gx', 'yz')), may hold values from 0 to 15, as said below
- owners: int32 [32, 12, 1], P(('gx', 'yz')), may hold values from 0 to 7; in each aligned block of 12 rows (0 to 11, 12 to 23, ..., all dimensions but the last counted through in order) at most 2 rows name the same one
- toughness: float32 [32, 8, 2, 8, 16, 128], P(('gx', 'yz')), may hold values from 0.5 to 2
Outputs:
- new_displacement: float32 [3, 32, 128, 2048], P(None, 'gx', 'yz')
- history: float32 [32, 128, 2048], P('gx', 'yz')
- new_damage: float32 [32, 128, 2048], P('gx', 'yz')
The draws below stay inside these ranges and needn't reach their ends.
Inputs may be any that keep to these rules, and one draw needn't show every extreme that they name: `owners`: the entries of one device name one owner at most 2 times, and exactly 2 times in some devices. `patch_ids`: the 12 entries of one device are distinct.
All inputs are finite; a program needn't handle non-finite values.
Results may differ from the reference program's by a relative error of at most 0.0001.
Values sent between devices are 32-bit elements; how exact they have to be, the bound alone decides.
No kernel may reach another device: no remote copies, remote signals or barrier semaphores. Data moves between devices by JAX's collectives and lax.ppermute only.
A program may use at most 128 MiB of HBM per device.

```python
import math
import jax
import jax.numpy as jnp
import numpy as np

CX = 8
CY = 16
CZ = 2048
PZ = 128
PL = 12
CAP = 2
MSTEPS = 2
SWEEPS = 8
PB = 16
NX = 32
NY = 128
N_GX = 4
N_YZ = 8
DEVICES = 32


def draw_patch_ids(key, part):
    keys = jax.random.split(key, DEVICES)
    orders = jax.vmap(lambda single: jax.random.permutation(single, CZ // PZ))(keys)
    return orders[:, :PL].astype(jnp.int32)


def touch_ends(drawn, own_key, low, top_value):
    place = [jax.random.randint(jax.random.fold_in(own_key, axis), (), 0, length) for axis, length in enumerate(drawn.shape)]
    widest = drawn.shape.index(max(drawn.shape))
    beside = place[:widest] + [(place[widest] + 1) % drawn.shape[widest]] + place[widest + 1:]
    return drawn.at[tuple(place)].set(low).at[tuple(beside)].set(top_value)


def block_scale(stream_key, dims, cuts, smallest, high):
    gain, own = 1.0, jax.random.fold_in(stream_key, 6)
    for axis_at, blocks in cuts:
        steps = jnp.exp(jax.random.uniform(jax.random.fold_in(own, axis_at), (blocks,), jnp.float32, smallest / len(cuts), high / len(cuts)))
        gain = gain * jnp.repeat(steps, dims[axis_at] // blocks).reshape([-1 if axis == axis_at else 1 for axis in range(len(dims))])
    return gain


def assign_block(stream_key, own, number, rows, count, top, most, lean):
    order = jax.random.permutation(stream_key, count)
    packed, ordinary = load_shares(count, rows * top, most, lean, True), load_shares(count, rows * top, most, lean, False)
    places = jnp.arange(count)

    def named(tallies, rotation):
        used = int((tallies > 0).sum())
        fixed = max(1, used // 4)
        passed = fixed + (places - fixed + rotation * (used - fixed)) % max(1, count - fixed)
        return jnp.zeros((count,), jnp.int32).at[order[jnp.where(places < fixed, places, passed)]].set(jnp.asarray(tallies, jnp.int32))

    tallies = jnp.where(number % 4 == 0, named(packed, number // 4), named(ordinary, number - number // 4 - 1))
    mixed = jax.random.permutation(jax.random.fold_in(own, 3), count)
    donor, receiver = mixed[0:count // 2 * 2:2], mixed[1:count // 2 * 2:2]
    slack = jnp.minimum(tallies[donor] - 1, most - tallies[receiver]) // 2
    slack = jnp.where((donor == order[0]) | (receiver == order[0]) | (tallies[receiver] == 0), 0, jnp.maximum(slack, 0))
    passed = jax.random.randint(jax.random.fold_in(own, 4), (count // 2,), 0, 1 << 20) % (slack + 1)
    tallies = tallies.at[donor].add(-passed).at[receiver].add(passed)
    labels = jnp.searchsorted(jnp.cumsum(tallies), jnp.arange(rows * top), side="right").astype(jnp.int32)
    grid = labels.reshape(top, rows).T
    grid = grid[jax.random.permutation(jax.random.fold_in(own, 1), rows)]
    rotation = jax.random.randint(jax.random.fold_in(own, 2), (rows, 1), 0, top)
    return jnp.take_along_axis(grid, (jnp.arange(top)[None, :] + rotation) % top, axis=1)


def load_shares(number_of, total, bound, skew, full):
    weights = [(1 << 20) // math.isqrt(standing ** skew) + 1 for standing in range(1, number_of + 1)]
    largest = bound if full else min(bound, max(-(-total // number_of), total * weights[0] // sum(weights)))
    least = 1 if total - largest >= number_of - 1 else 0
    counts, spare = [largest] + [least] * (number_of - 1), total - largest - least * (number_of - 1)
    while spare > 0:
        free = [i for i in range(1, number_of) if counts[i] < largest] or [i for i in range(1, number_of) if counts[i] < bound]
        pool, left = sum([weights[i] for i in free]), spare
        for i in free:
            addition = min(bound - counts[i], max(1, left * weights[i] // pool), spare)
            counts[i] = counts[i] + addition
            spare = spare - addition
    return np.array(counts)


def noise(rng, extent, scale, limit, pieces=(), held_as=jnp.bfloat16):
    loudness = block_scale(rng, extent, pieces, -0.22, 0.18) if pieces else 1.0
    array = jax.random.normal(rng, extent, jnp.float32) * scale * loudness
    return jnp.minimum(jnp.maximum(array, -limit), limit).astype(held_as)


def setup_inputs(seed: int = 0) -> dict:
    arg_keys = jax.random.split(jax.random.key(seed), 9)
    displacement = noise(arg_keys[0], (3, NX, NY, CZ), 0.2, 1.2, ((1, 4), (2, 8)), jnp.float32)
    force = noise(arg_keys[1], (3, NX, NY, CZ), 0.2, 1.2, ((1, 4), (2, 8)), jnp.float32)
    damage = jnp.clip(0.6 * jax.random.uniform(arg_keys[2], (NX, NY, CZ), jnp.float32) ** block_scale(arg_keys[2], (NX, NY, CZ), ((0, 4), (1, 8)), -0.2, 0.2), 0.0, 0.6)
    history_old = jnp.clip(0.5 * jax.random.uniform(arg_keys[3], (NX, NY, CZ), jnp.float32) ** block_scale(arg_keys[3], (NX, NY, CZ), ((0, 4), (1, 8)), -0.2, 0.2), 0.0, 0.5)
    material = touch_ends(jax.random.randint(arg_keys[4], (NX, NY, CZ), 0, 4), jax.random.fold_in(arg_keys[4], 1), 0, 3).astype(jnp.int32)
    patch_ids = draw_patch_ids(jax.random.fold_in(arg_keys[8], 71), 0)
    owners_keys = jax.random.split(jax.random.fold_in(arg_keys[6], 1), DEVICES * PL // PL)
    owners_turns = jax.random.permutation(jax.random.fold_in(arg_keys[6], 3), DEVICES * PL // PL)
    owners = jax.vmap(lambda own, number: assign_block(jax.random.fold_in(arg_keys[6], 2), own, number, PL, N_YZ, 1, CAP, 2))(owners_keys, owners_turns).reshape((DEVICES, PL, 1))
    toughness = jnp.clip(jnp.exp(math.log(2.0) - 1.3862944 * jax.random.uniform(arg_keys[7], (DEVICES, N_YZ, CAP, CX, CY, PZ), jnp.float32) ** block_scale(arg_keys[7], (DEVICES, N_YZ, CAP, CX, CY, PZ), ((0, 32),), -0.2, 0.2)), 0.5, 2.0)
    return dict(displacement=displacement, force=force, damage=damage, history_old=history_old, material=material, patch_ids=patch_ids, owners=owners, toughness=toughness)


MODULI = (1.0, 0.5, 4.0, 0.25)
SPRING = 0.05
RELAX = 0.8
LENGTH = 2.0


def modulus(material):
    result = jnp.zeros(material.shape, jnp.float32)
    for index, value in enumerate(MODULI):
        result = result + jnp.where(material == index, jnp.float32(value), jnp.float32(0.0))
    return result


def adjacent(padded):
    return [padded[..., 2:, 1:-1, 1:-1], padded[..., :-2, 1:-1, 1:-1],
            padded[..., 1:-1, 2:, 1:-1], padded[..., 1:-1, :-2, 1:-1],
            padded[..., 1:-1, 1:-1, 2:], padded[..., 1:-1, 1:-1, :-2]]


def zero_pad(field):
    widths = [(0, 0)] * (field.ndim - 3) + [(1, 1)] * 3
    return jnp.pad(field, widths)


def sweep(hist, start, tough):
    first = tough / LENGTH + 2.0 * hist
    second = tough * LENGTH
    denom = first + 6.0 * second
    value = start
    widths = [(0, 0)] * (value.ndim - 3) + [(1, 1)] * 3
    for step in range(SWEEPS):
        padded = jnp.pad(value, widths, mode="edge")
        total = sum(adjacent(padded))
        value = (2.0 * hist + second * total) / denom
    return jnp.maximum(value, start)


def to_patches(field):
    parts = field.reshape(N_GX, CX, N_YZ, CY, PB, PZ).transpose(0, 2, 4, 1, 3, 5)
    return parts.reshape(N_GX * N_YZ, PB, CX, CY, PZ)


def from_patches(parts):
    parts = parts.reshape(N_GX, N_YZ, PB, CX, CY, PZ).transpose(0, 3, 1, 4, 2, 5)
    return parts.reshape(N_GX * CX, N_YZ * CY, PB * PZ)


def reference(displacement, force, damage, history_old, material, patch_ids, owners, toughness):
    moduli = modulus(material)
    stiffness = moduli * ((1.0 - damage) ** 2 + 0.001)
    weights = [0.5 * (stiffness + other) for other in adjacent(zero_pad(stiffness))]
    diag = SPRING * stiffness + sum(weights)
    field = displacement
    for step in range(MSTEPS):
        near = adjacent(zero_pad(field))
        applied = SPRING * stiffness * field
        for weight, other in zip(weights, near):
            applied = applied + weight * (field - other)
        field = field + RELAX * (force - applied) / diag
    near = adjacent(zero_pad(field))
    squares = (near[0] - field) ** 2 + (near[2] - field) ** 2 + (near[4] - field) ** 2
    energy = 0.5 * moduli * jnp.sum(squares, axis=0)
    history = jnp.maximum(history_old, energy)
    owner_of = owners[:, :, 0]
    earlier = jnp.arange(PL)[None, :] < jnp.arange(PL)[:, None]
    same = owner_of[:, :, None] == owner_of[:, None, :]
    slot_rank = jnp.sum(jnp.where(same & earlier[None], 1, 0), axis=2).astype(jnp.int32)
    devices = jnp.arange(N_GX * N_YZ).astype(jnp.int32)
    source_yz = devices % N_YZ
    owner_dev = (devices // N_YZ)[:, None] * N_YZ + owner_of
    tough = toughness[owner_dev, source_yz[:, None], slot_rank]
    hist_parts = to_patches(history)[devices[:, None], patch_ids]
    damage_all = to_patches(damage)
    start = damage_all[devices[:, None], patch_ids]
    result = sweep(hist_parts, start, tough)
    damage_all = damage_all.at[devices[:, None], patch_ids].set(result)
    return field, history, from_patches(damage_all)
```

```python
import functools

import jax
import jax.numpy as jnp
from jax import lax
from jax.experimental import pallas as pl
from jax.experimental.pallas import tpu as pltpu
from jax.sharding import PartitionSpec as P

MSTEPS = 2
SWEEPS = 8
MODULI = (1.0, 0.5, 4.0, 0.25)
SPRING = 0.05
RELAX = 0.8
LENGTH = 2.0
ROWS = 8
LANES = 128
GRANT = 40 * 1024 * 1024

VMEM = pltpu.MemorySpace.VMEM
F32 = jnp.float32


def resident(shape):
    return pltpu.VMEM(shape, F32)


def plain(shape):
    return jax.ShapeDtypeStruct(shape, F32)


def held(value):
    return pltpu.with_memory_space_constraint(value, VMEM)


def modulus(material):
    low = jnp.where(material == 0, MODULI[0], MODULI[1])
    high = jnp.where(material == 2, MODULI[2], MODULI[3])
    return jnp.where(material < 2, low, high)


def lane_index():
    return lax.broadcasted_iota(jnp.int32, (ROWS, LANES), 1)


def row_index():
    return lax.broadcasted_iota(jnp.int32, (ROWS, LANES), 0)


def tile(ref, lead, t, k):
    return ref[(*lead, slice(t * ROWS, (t + 1) * ROWS), slice(k * LANES, (k + 1) * LANES))]


def put(ref, lead, t, k, value):
    ref[(*lead, slice(t * ROWS, (t + 1) * ROWS), slice(k * LANES, (k + 1) * LANES))] = value


def halo_row(ref, lead, x, k, place):
    value = ref[(*lead, slice(0, ROWS), slice(k * LANES, (k + 1) * LANES))]
    return pltpu.roll(value, (place - x + ROWS) % ROWS, 0)


def z_next(tiles, row, ends):
    lane = lane_index()
    rolled = [pltpu.roll(v, LANES - 1, 1) for v in tiles]
    after = rolled[1:] + [rolled[0] if ends is None else ends]
    return [jnp.where(lane == LANES - 1, b, a) for a, b in zip(rolled, after)]


def z_prev(tiles, row, ends):
    lane = lane_index()
    rolled = [pltpu.roll(v, 1, 1) for v in tiles]
    before = [rolled[-1] if ends is None else ends] + rolled[:-1]
    return [jnp.where(lane == 0, b, a) for a, b in zip(rolled, before)]


def y_prev(column, low):
    row = row_index()
    rolled = [pltpu.roll(v, 1, 0) for v in column]
    before = [low] + rolled[:-1]
    return [jnp.where(row == 0, b, a) for a, b in zip(rolled, before)]


def y_next(column, high):
    row = row_index()
    rolled = [pltpu.roll(v, ROWS - 1, 0) for v in column]
    after = rolled[1:] + [high]
    return [jnp.where(row == ROWS - 1, b, a) for a, b in zip(rolled, after)]


def pack_y(read, out_low, out_high, count, nx, ny):
    for c in range(count):
        for x in range(nx):
            out_low[c, x : x + 1, :] = read(c, x, 0)
            out_high[c, x : x + 1, :] = read(c, x, ny - 1)


def parities():
    return lax.axis_index("gx") % 2, lax.axis_index("yz") % 2


def by_parity(parity, even, odd, then):
    @pl.when(parity == 0)
    def _():
        then(odd, even)

    @pl.when(parity == 1)
    def _():
        then(even, odd)


def pick(parity, even, odd):
    return jnp.where(parity == 0, odd, even), jnp.where(parity == 0, even, odd)


def pack_faces(field, extra, xe, xo, ye, yo):
    _, nx, ny, nz = field.shape
    px, py = parities()

    def planes(low, high):
        low[0:3] = field[:, 0]
        high[0:3] = field[:, nx - 1]
        if extra is not None:
            low[3] = extra[0]
            high[3] = extra[nx - 1]

    def rows(low, high):
        pack_y(lambda c, x, y: field[c, x, y : y + 1, :], low, high, 3, nx, ny)
        if extra is not None:
            for x in range(nx):
                low[3, x : x + 1, :] = extra[x, 0:1, :]
                high[3, x : x + 1, :] = extra[x, ny - 1 : ny, :]

    by_parity(px, xe, xo, planes)
    by_parity(py, ye, yo, rows)


def begin_kernel(damage, material, field, stiff, u_keep, xe, xo, ye, yo):
    nx, ny, nz = damage.shape

    def plane(x, _):
        d = damage[x]
        stiff[x] = modulus(material[x]) * ((1.0 - d) * (1.0 - d) + 0.001)
        for c in range(3):
            u_keep[c, x] = field[c, x]
        return 0

    lax.fori_loop(0, nx, plane, 0)
    pack_faces(field, stiff, xe, xo, ye, yo)


def step_plane(x, u, coef, load, u_low, u_high, y_low, y_high, out):
    nt, nk = u.shape[2] // ROWS, u.shape[3] // LANES
    for c in range(3):
        tiles = [[tile(u, (c, x), t, k) for k in range(nk)] for t in range(nt)]
        zn = [z_next(r, t, None) for t, r in enumerate(tiles)]
        zp = [z_prev(r, t, None) for t, r in enumerate(tiles)]
        for k in range(nk):
            column = [tiles[t][k] for t in range(nt)]
            yp = y_prev(column, y_low(c, x, k))
            yn = y_next(column, y_high(c, x, k))
            for t in range(nt):
                cs = [tile(coef, (i, x), t, k) for i in range(6)]
                total = cs[0] * u_high(c, t, k) + cs[1] * u_low(c, t, k)
                total = total + (cs[2] * yn[t] + cs[3] * yp[t])
                total = total + (cs[4] * zn[t][k] + cs[5] * zp[t][k])
                total = total + load(c, x, t, k)
                put(out, (c, x), t, k, (1.0 - RELAX) * column[t] + total)


def planes_of(nx, body):
    body(0, -1)

    def inner(x, _):
        body(x, 0)
        return 0

    lax.fori_loop(1, nx - 1, inner, 0)
    body(nx - 1, 1)


def fill_halo(hxe, hxo, hye, hyo, hx, hy):
    px, py = parities()
    count = hxe.shape[0]
    for c in range(count):
        hx[0, c], hx[1, c] = pick(px, hxe[c], hxo[c])
        hy[0, c], hy[1, c] = pick(py, hye[c], hyo[c])


def neighbours_x(ref, hx, c_halo, lead):
    nx = ref.shape[len(lead)]

    def make(x, place):
        def low(t, k):
            return tile(hx, (0, c_halo), t, k) if place == -1 else tile(ref, (*lead, x - 1), t, k)

        def high(t, k):
            return tile(hx, (1, c_halo), t, k) if place == 1 else tile(ref, (*lead, x + 1), t, k)

        return low, high

    return make


def run_step(u, hx, hy, coef, load, out):
    nx = u.shape[1]

    def body(x, place):
        makers = [neighbours_x(u, hx, c, (c,))(x, place) for c in range(3)]
        step_plane(
            x, u, coef, load,
            lambda c, t, k: makers[c][0](t, k),
            lambda c, t, k: makers[c][1](t, k),
            lambda c, x, k: halo_row(hy, (0, c), x, k, 0),
            lambda c, x, k: halo_row(hy, (1, c), x, k, ROWS - 1),
            out,
        )

    planes_of(nx, body)


def first_kernel(u, stiff, force, hxe, hxo, hye, hyo, coef, load, out, xe, xo, ye, yo, hx, hy):
    nx, ny, nz = stiff.shape
    nt, nk = ny // ROWS, nz // LANES
    fill_halo(hxe, hxo, hye, hyo, hx, hy)

    def body(x, place):
        lane = lane_index()
        low, high = neighbours_x(stiff, hx, 3, ())(x, place)
        tiles = [[tile(stiff, (x,), t, k) for k in range(nk)] for t in range(nt)]
        zero = jnp.zeros((ROWS, LANES), F32)
        zn = [z_next(r, t, zero) for t, r in enumerate(tiles)]
        zp = [z_prev(r, t, zero) for t, r in enumerate(tiles)]
        for k in range(nk):
            column = [tiles[t][k] for t in range(nt)]
            yp = y_prev(column, halo_row(hy, (0, 3), x, k, 0))
            yn = y_next(column, halo_row(hy, (1, 3), x, k, ROWS - 1))
            for t in range(nt):
                s = column[t]
                others = [high(t, k), low(t, k), yn[t], yp[t], zn[t][k], zp[t][k]]
                weights = [0.5 * (s + o) for o in others]
                diag = SPRING * s + sum(weights)
                scale = RELAX / diag
                for i, w in enumerate(weights):
                    value = scale * w
                    if i == 4 and k == nk - 1:
                        value = jnp.where(lane == LANES - 1, 0.0, value)
                    if i == 5 and k == 0:
                        value = jnp.where(lane == 0, 0.0, value)
                    put(coef, (i, x), t, k, value)
                for c in range(3):
                    put(load, (c, x), t, k, scale * tile(force, (c, x), t, k))

    planes_of(nx, body)
    run_step(u, hx, hy, coef, lambda c, x, t, k: tile(load, (c, x), t, k), out)
    pack_faces(out, None, xe, xo, ye, yo)


def second_kernel(u, coef, load, hxe, hxo, hye, hyo, out, xlow, ylow, hx, hy):
    nx, ny = u.shape[1:3]
    fill_halo(hxe, hxo, hye, hyo, hx, hy)
    run_step(u, hx, hy, coef, lambda c, x, t, k: tile(load, (c, x), t, k), out)
    xlow[...] = out[:, 0]
    for c in range(3):
        for x in range(nx):
            ylow[c, x : x + 1, :] = out[c, x, 0:1, :]


def last_kernel(ids, owners, u, material, history_old, damage, tough, hx, hy, history, new_damage):
    nx, ny, nz = damage.shape
    nt, nk = ny // ROWS, nz // LANES

    def body(x, place):
        lane = lane_index()
        squares = {}
        for c in range(3):
            _, high = neighbours_x(u, None, c, (c,))(x, 0)
            tiles = [[tile(u, (c, x), t, k) for k in range(nk)] for t in range(nt)]
            zero = jnp.zeros((ROWS, LANES), F32)
            zn = [z_next(r, t, zero) for t, r in enumerate(tiles)]
            for k in range(nk):
                column = [tiles[t][k] for t in range(nt)]
                yn = y_next(column, halo_row(hy, (c,), x, k, ROWS - 1))
                for t in range(nt):
                    v = column[t]
                    after = tile(hx, (c,), t, k) if place == 1 else high(t, k)
                    a, b, d = after - v, yn[t] - v, zn[t][k] - v
                    total = a * a + b * b + d * d
                    squares[t, k] = total if c == 0 else squares[t, k] + total
        for k in range(nk):
            for t in range(nt):
                energy = 0.5 * modulus(tile(material, (x,), t, k)) * squares[t, k]
                put(history, (x,), t, k, jnp.maximum(tile(history_old, (x,), t, k), energy))
                put(new_damage, (x,), t, k, tile(damage, (x,), t, k))

    planes_of(nx, body)

    count = ids.shape[1]

    def patch(j, _):
        lane, row = lane_index(), row_index()
        owner = owners[0, j]
        slot = lax.fori_loop(0, j, lambda i, n: n + (owners[0, i] == owner).astype(jnp.int32), jnp.int32(0))
        start = pl.multiple_of(ids[0, j] * LANES, LANES)
        cells = [(x, t) for x in range(nx) for t in range(nt)]

        def at(ref, x, t):
            return ref[x, t * ROWS : (t + 1) * ROWS, pl.ds(start, LANES)]

        first, second, d = {}, {}, {}
        for x, t in cells:
            h2 = 2.0 * at(history, x, t)
            g = tough[owner, slot, x, t * ROWS : (t + 1) * ROWS, :]
            g2 = g * LENGTH
            inverse = 1.0 / (g / LENGTH + h2 + 6.0 * g2)
            first[x, t] = h2 * inverse
            second[x, t] = g2 * inverse
            d[x, t] = at(damage, x, t)
        for _ in range(SWEEPS):
            new = {}
            for x in range(nx):
                column = [d[x, t] for t in range(nt)]
                yp = y_prev(column, column[0])
                yn = y_next(column, column[-1])
                for t in range(nt):
                    v = column[t]
                    zn = jnp.where(lane == LANES - 1, v, pltpu.roll(v, LANES - 1, 1))
                    zp = jnp.where(lane == 0, v, pltpu.roll(v, 1, 1))
                    total = (d[min(x + 1, nx - 1), t] + d[max(x - 1, 0), t]) + (yn[t] + yp[t]) + (zn + zp)
                    new[x, t] = first[x, t] + second[x, t] * total
            d = new
        for x, t in cells:
            new_damage[x, t * ROWS : (t + 1) * ROWS, pl.ds(start, LANES)] = jnp.maximum(d[x, t], at(damage, x, t))
        return 0

    lax.fori_loop(0, count, patch, 0)


def swaps(axis, first):
    size = lax.axis_size(axis)
    pairs = [(i, i + 1) for i in range(first, size - 1, 2)]
    return pairs + [(b, a) for a, b in pairs]


def exchange(xe, xo, ye, yo):
    return (
        lax.ppermute(xe, "gx", swaps("gx", 0)),
        lax.ppermute(xo, "gx", swaps("gx", 1)),
        lax.ppermute(ye, "yz", swaps("yz", 0)),
        lax.ppermute(yo, "yz", swaps("yz", 1)),
    )


def from_above(value, axis):
    size = lax.axis_size(axis)
    return lax.ppermute(value, axis, [(i + 1, i) for i in range(size - 1)])


def call(kernel, outs, scratch=(), smem=0, count=0):
    specs = [pl.BlockSpec(memory_space=pltpu.SMEM)] * smem + [pl.BlockSpec(memory_space=VMEM)] * count
    return pl.pallas_call(
        kernel,
        out_shape=outs,
        in_specs=specs,
        out_specs=[pl.BlockSpec(memory_space=VMEM)] * len(outs),
        scratch_shapes=scratch,
        compiler_params=pltpu.CompilerParams(vmem_limit_bytes=GRANT),
    )


def body(displacement, force, damage, history_old, material, patch_ids, owners, toughness):
    nx, ny, nz = damage.shape
    full, cells = (3, nx, ny, nz), (nx, ny, nz)

    def faces(count):
        return [plain((count, ny, nz))] * 2 + [plain((count, nx, nz))] * 2

    def halos(count):
        return [pltpu.VMEM((2, count, ny, nz), F32), pltpu.VMEM((2, count, nx, nz), F32)]

    arrived = lax.all_to_all(toughness[0], "yz", split_axis=0, concat_axis=0, tiled=True)
    stiff, u, *sent = call(begin_kernel, [resident(cells), resident(full)] + faces(4), count=3)(damage, material, displacement)
    brought = exchange(*sent)
    coef, load, u, *sent = call(
        first_kernel, [resident((6,) + cells), resident(full), resident(full)] + faces(3), halos(4), count=7
    )(held(u), held(stiff), force, *brought)
    brought = exchange(*sent)
    u, xlow, ylow = call(second_kernel, [resident(full), plain((3, ny, nz)), plain((3, nx, nz))], halos(3), count=7)(
        held(u), held(coef), held(load), *brought
    )
    history, new_damage = call(last_kernel, [plain(cells)] * 2, smem=2, count=7)(
        patch_ids, owners[:, :, 0], held(u), material, history_old, damage, arrived, from_above(xlow, "gx"), from_above(ylow, "yz")
    )
    return (u, history, new_damage)


def solution(mesh):
    return jax.shard_map(
        body,
        mesh=mesh,
        in_specs=(
            P(None, "gx", "yz", None),
            P(None, "gx", "yz", None),
            P("gx", "yz", None),
            P("gx", "yz", None),
            P("gx", "yz", None),
            P(("gx", "yz"), None),
            P(("gx", "yz"), None, None),
            P(("gx", "yz"), None, None, None, None, None),
        ),
        out_specs=(P(None, "gx", "yz", None), P("gx", "yz", None), P("gx", "yz", None)),
        check_vma=False,
    )
```

```python
import jax
import jax.numpy as jnp
from jax import lax
from jax.experimental import pallas as pl
from jax.experimental.pallas import tpu as pltpu
from jax.sharding import PartitionSpec as P

SWEEPS = 8
MODULI = (1.0, 0.5, 4.0, 0.25)
SPRING = 0.05
RELAX = 0.8
LENGTH = 2.0
ROWS = 8
LANES = 128
LOW, HIGH = 0, 1
GRANT = 8 * 1024 * 1024

VMEM = pltpu.MemorySpace.VMEM
HBM = pltpu.MemorySpace.HBM
F32 = jnp.float32


def modulus(material):
    low = jnp.where(material == 0, MODULI[0], MODULI[1])
    high = jnp.where(material == 2, MODULI[2], MODULI[3])
    return jnp.where(material < 2, low, high)


def lane_index():
    return lax.broadcasted_iota(jnp.int32, (ROWS, LANES), 1)


def row_index():
    return lax.broadcasted_iota(jnp.int32, (ROWS, LANES), 0)


def where_tile(lead, t, k):
    return (*lead, slice(t * ROWS, (t + 1) * ROWS), slice(k * LANES, (k + 1) * LANES))


def tile(ref, lead, t, k):
    return ref[where_tile(lead, t, k)]


def put(ref, lead, t, k, value):
    ref[where_tile(lead, t, k)] = value


def moved(value, source, target):
    shift = (target - source) % ROWS if isinstance(source, int) else (target - source + ROWS) % ROWS
    if isinstance(shift, int) and shift == 0:
        return value
    return pltpu.roll(value, shift, 0)


class Line:
    def __init__(self, load, nk):
        self.load, self.nk, self.kept = load, nk, {}

    def get(self, kind, k):
        k = k % self.nk
        if (kind, k) not in self.kept:
            if kind == "own":
                value = self.load(k)
            else:
                value = pltpu.roll(self.get("own", k), LANES - 1 if kind == "next" else 1, 1)
            self.kept[kind, k] = value
        return self.kept[kind, k]

    def own(self, k):
        return self.get("own", k)

    def after(self, k):
        return jnp.where(lane_index() == LANES - 1, self.get("next", k + 1), self.get("next", k))

    def before(self, k):
        return jnp.where(lane_index() == 0, self.get("prev", k - 1), self.get("prev", k))


def y_before(column):
    rolled = [pltpu.roll(v, 1, 0) for v in column]
    row = row_index()
    return rolled[:1] + [jnp.where(row == 0, a, b) for a, b in zip(rolled, rolled[1:])]


def y_after(column):
    rolled = [pltpu.roll(v, ROWS - 1, 0) for v in column]
    row = row_index()
    return [jnp.where(row == ROWS - 1, b, a) for a, b in zip(rolled, rolled[1:])] + rolled[-1:]


def by_parity(parity, even, odd, then):
    @pl.when(parity == 0)
    def _():
        then(odd, even)

    @pl.when(parity == 1)
    def _():
        then(even, odd)


class Halo:
    def __init__(self, axis, even, odd):
        place, size = lax.axis_index(axis), lax.axis_size(axis)
        self.even, self.odd = even, odd
        self.parity = place % 2
        self.inside = (place > 0, place < size - 1)

    def get(self, side, load):
        even, odd = load(self.even), load(self.odd)
        here = self.parity == (1 if side == LOW else 0)
        return jnp.where(self.inside[side], jnp.where(here, even, odd), 0.0)


def planes_of(nx, body):
    body(0, -1)

    def inner(x, _):
        body(x, 0)
        return 0

    lax.fori_loop(1, nx - 1, inner, 0)
    body(nx - 1, 1)


def start_all(copies):
    for copy in copies:
        copy.start()


def pack_planes(even, odd, read, nx, nt):
    def planes(low, high):
        for side, out in ((0, low), (nx - 1, high)):
            for t in range(nt):
                for c in range(out.shape[0]):
                    out[c, t * ROWS : (t + 1) * ROWS, :] = read(c, side, t)

    by_parity(lax.axis_index("gx") % 2, even, odd, planes)


def begin_kernel(damage, material, field, u, stiff, ye, yo, xe, xo, damage_kept, material_kept, sems):
    nx, ny, nz = stiff.shape
    nt = ny // ROWS
    copies = [
        pltpu.make_async_copy(damage, damage_kept, sems.at[0]),
        pltpu.make_async_copy(material, material_kept, sems.at[1]),
        pltpu.make_async_copy(field, u, sems.at[2]),
    ]
    start_all(copies)
    copies[0].wait()
    copies[1].wait()

    def plane(x, _):
        d = 1.0 - damage_kept[x]
        stiff[x] = modulus(material_kept[x]) * (d * d + 0.001)
        return 0

    lax.fori_loop(0, nx, plane, 0)
    copies[2].wait()

    def rows(low, high):
        for side, out in ((0, low), (ny - 1, high)):
            for x in range(nx):
                for c in range(3):
                    out[c, x : x + 1, :] = u[c, x, side : side + 1, :]
                out[3, x : x + 1, :] = stiff[x, side : side + 1, :]

    by_parity(lax.axis_index("yz") % 2, ye, yo, rows)

    def read(c, x, t):
        part = slice(t * ROWS, (t + 1) * ROWS)
        return u[c, x, part, :] if c < 3 else stiff[x, part, :]

    pack_planes(xe, xo, read, nx, nt)


def relax_inner(x, place, u, load, weights, scale, out, acc_x, acc_y, faces):
    nt, nk = u.shape[2] // ROWS, u.shape[3] // LANES
    lines = {(c, t): Line(lambda k, c=c, t=t: tile(u, (c, x), t, k), nk) for c in range(3) for t in range(nt)}
    for k in range(nk):
        found = [weights(x, t, k) for t in range(nt)]
        scales = [scale(x, t, k) for t in range(nt)]
        for c in range(3):
            column = [lines[c, t].own(k) for t in range(nt)]
            yb, ya = y_before(column), y_after(column)
            for t in range(nt):
                xh, xl, wya, wyb, wza, wzb = found[t]
                total = load(c, x, t, k)
                if place != 1:
                    total = total + xh * tile(u, (c, x + 1), t, k)
                if place != -1:
                    total = total + xl * tile(u, (c, x - 1), t, k)
                total = total + (wya * ya[t] + wyb * yb[t])
                total = total + (wza * lines[c, t].after(k) + wzb * lines[c, t].before(k))
                if place == -1:
                    put(acc_x, (LOW, c), t, k, total)
                if place == 1:
                    put(acc_x, (HIGH, c), t, k, total)
                if t == 0:
                    put(faces, (LOW, c, x), 0, k, total)
                if t == nt - 1:
                    put(faces, (HIGH, c, x), 0, k, total)
                put(out, (c, x), t, k, (1.0 - RELAX) * column[t] + scales[t] * total)


def compact_rows(faces, out, nx):
    for c in range(out.shape[1]):
        for x in range(nx):
            out[LOW, c, x : x + 1, :] = faces[LOW, c, x, 0:1, :]
            out[HIGH, c, x : x + 1, :] = faces[HIGH, c, x, ROWS - 1 : ROWS, :]


def inner_one_kernel(
    u, stiff, force, wx, wya, wyb, wza, wzb, scale, out, acc_x, acc_y, diag_x, diag_y, faces, diag_faces
):
    nx, ny, nz = stiff.shape
    nt, nk = ny // ROWS, nz // LANES

    def prepare(x, place):
        lane, row = lane_index(), row_index()
        lines = [Line(lambda k, t=t: tile(stiff, (x,), t, k), nk) for t in range(nt)]
        for k in range(nk):
            column = [lines[t].own(k) for t in range(nt)]
            yb, ya = y_before(column), y_after(column)
            for t in range(nt):
                s = column[t]
                half = 0.5 * s
                diag = SPRING * s
                if place != 1:
                    w = half + 0.5 * tile(stiff, (x + 1,), t, k)
                    put(wx, (x,), t, k, w)
                    diag = diag + w
                if place != -1:
                    diag = diag + (half + 0.5 * tile(stiff, (x - 1,), t, k))
                w = half + 0.5 * ya[t]
                if t == nt - 1:
                    w = jnp.where(row == ROWS - 1, 0.0, w)
                put(wya, (x,), t, k, w)
                diag = diag + w
                w = half + 0.5 * yb[t]
                if t == 0:
                    w = jnp.where(row == 0, 0.0, w)
                put(wyb, (x,), t, k, w)
                diag = diag + w
                w = half + 0.5 * lines[t].after(k)
                if k == nk - 1:
                    diag = diag + jnp.where(lane == LANES - 1, half, w)
                    w = jnp.where(lane == LANES - 1, 0.0, w)
                else:
                    diag = diag + w
                put(wza, (x,), t, k, w)
                w = half + 0.5 * lines[t].before(k)
                if k == 0:
                    diag = diag + jnp.where(lane == 0, half, w)
                    w = jnp.where(lane == 0, 0.0, w)
                else:
                    diag = diag + w
                put(wzb, (x,), t, k, w)
                put(scale, (x,), t, k, RELAX / diag)
                if place == -1:
                    put(diag_x, (LOW,), t, k, diag)
                if place == 1:
                    put(diag_x, (HIGH,), t, k, diag)
                if t == 0:
                    put(diag_faces, (LOW, 0, x), 0, k, diag)
                if t == nt - 1:
                    put(diag_faces, (HIGH, 0, x), 0, k, diag)

    planes_of(nx, prepare)
    inner_pass(u, force, wx, wya, wyb, wza, wzb, scale, out, acc_x, acc_y, faces)
    compact_rows(diag_faces, diag_y, nx)


def inner_pass(u, force, wx, wya, wyb, wza, wzb, scale, out, acc_x, acc_y, faces):
    nx = u.shape[1]

    def body(x, place):
        def weights(x, t, k):
            high = None if place == 1 else tile(wx, (x,), t, k)
            low = None if place == -1 else tile(wx, (x - 1,), t, k)
            return (high, low) + tuple(tile(w, (x,), t, k) for w in (wya, wyb, wza, wzb))

        relax_inner(
            x, place, u, lambda c, x, t, k: tile(force, (c, x), t, k), weights, lambda x, t, k: tile(scale, (x,), t, k), out,
            acc_x, acc_y, faces,
        )

    planes_of(nx, body)
    compact_rows(faces, acc_y, nx)


def x_part(value, c, t, k):
    return tile(value[t], (c,), 0, k) if isinstance(value, tuple) else tile(value, (c,), t, k)


def own_side(parity, side, sent_even, sent_odd, lead, k):
    even, odd = tile(sent_even, lead, 0, k), tile(sent_odd, lead, 0, k)
    return jnp.where(parity == (1 if side == LOW else 0), even, odd)


def face_one_kernel(
    u, stiff, sye, syo, acc_x, acc_y, diag_x, diag_y, hye, hyo, hxe, hxo,
    ye, yo, xe, xo, w_x, w_xy, s_x, w_y, w_yx, s_y, planes,
):
    _, nx, ny, nz = u.shape
    nt, nk = ny // ROWS, nz // LANES
    hy = Halo("yz", hye, hyo)
    hx = Halo("gx", hxe, hxo)
    row = row_index()

    def x_halo(side, c, t, k):
        return hx.get(side, lambda value: x_part(value, c, t, k))

    def y_halo(side, c, k):
        return hy.get(side, lambda ref: tile(ref, (c,), 0, k))

    def y_faces(even, odd):
        for side, out in ((LOW, odd), (HIGH, even)):
            y_row, t = (0, 0) if side == LOW else (ROWS - 1, nt - 1)
            for k in range(nk):
                own = own_side(hy.parity, side, sye, syo, (3,), k)
                w = 0.5 * (own + y_halo(side, 3, k))
                low = moved(x_halo(LOW, 3, t, k), y_row, 0)
                high = moved(x_halo(HIGH, 3, t, k), y_row, ROWS - 1)
                edge = jnp.where(row == 0, low, high)
                we = jnp.where((row == 0) | (row == ROWS - 1), 0.5 * (own + edge), 0.0)
                scale = RELAX / (tile(diag_y, (side, 0), 0, k) + w + we)
                put(w_y, (side,), 0, k, w)
                put(w_yx, (side,), 0, k, we)
                put(s_y, (side,), 0, k, scale)
                for c in range(3):
                    low = moved(x_halo(LOW, c, t, k), y_row, 0)
                    high = moved(x_halo(HIGH, c, t, k), y_row, ROWS - 1)
                    edge = jnp.where(row == 0, low, high)
                    total = tile(acc_y, (side, c), 0, k) + w * y_halo(side, c, k) + we * edge
                    own_u = own_side(hy.parity, side, sye, syo, (c,), k)
                    put(out, (c,), 0, k, (1.0 - RELAX) * own_u + scale * total)

    by_parity(hy.parity, ye, yo, lambda low, high: y_faces(high, low))

    for side in (LOW, HIGH):
            x = 0 if side == LOW else nx - 1
            for k in range(nk):
                for t in range(nt):
                    own = tile(stiff, (x,), t, k)
                    w = 0.5 * (own + x_halo(side, 3, t, k))
                    diag = tile(diag_x, (side,), t, k) + w
                    edge_side = LOW if t == 0 else HIGH if t == nt - 1 else None
                    if edge_side is not None:
                        y_row = 0 if t == 0 else ROWS - 1
                        we = 0.5 * (own + moved(y_halo(edge_side, 3, k), x, y_row))
                        we = jnp.where(row == y_row, we, 0.0)
                        diag = diag + we
                        put(w_xy, (side,), t, k, we)
                    scale = RELAX / diag
                    put(w_x, (side,), t, k, w)
                    put(s_x, (side,), t, k, scale)
                    for c in range(3):
                        total = tile(acc_x, (side, c), t, k) + w * x_halo(side, c, t, k)
                        if edge_side is not None:
                            total = total + we * moved(y_halo(edge_side, c, k), x, y_row)
                        value = (1.0 - RELAX) * tile(u, (c, x), t, k) + scale * total
                        put(planes, (side, c), t, k, value)

    def read(c, x, t):
        return planes[LOW if x == 0 else HIGH, c, t * ROWS : (t + 1) * ROWS, :]

    pack_planes(xe, xo, read, nx, nt)


def insert_faces(u, x_face, y_face):
    _, nx, ny, nz = u.shape
    nt, nk = ny // ROWS, nz // LANES
    for side, x in ((LOW, 0), (HIGH, nx - 1)):
        for c in range(3):
            for t in range(nt):
                for k in range(nk):
                    put(u, (c, x), t, k, x_face(side, c, t, k))

    def inner(x, _):
        row = row_index()
        for side, t, place in ((LOW, 0, 0), (HIGH, nt - 1, ROWS - 1)):
            for c in range(3):
                for k in range(nk):
                    value = moved(y_face(side, c, k), x, place)
                    put(u, (c, x), t, k, jnp.where(row == place, value, tile(u, (c, x), t, k)))
        return 0

    lax.fori_loop(1, nx - 1, inner, 0)


def inner_two_kernel(
    u_in, scale, force, wx, wya, wyb, wza, wzb, sye, syo, planes,
    u, out, acc_x, acc_y, faces,
):
    hy = lax.axis_index("yz") % 2
    insert_faces(u, lambda side, c, t, k: tile(planes, (side, c), t, k), lambda side, c, k: own_side(hy, side, sye, syo, (c,), k))
    inner_pass(u, force, wx, wya, wyb, wza, wzb, scale, out, acc_x, acc_y, faces)


def face_two_kernel(
    u, sye, syo, acc_x, acc_y, w_x, w_xy, s_x, w_y, w_yx, s_y, hye, hyo, hxe, hxo,
    x_low0, x_low1, y_low, x_high, y_high,
):
    _, nx, ny, nz = u.shape
    nt, nk = ny // ROWS, nz // LANES
    hy = Halo("yz", hye, hyo)
    hx = Halo("gx", hxe, hxo)
    row = row_index()

    def x_halo(side, c, t, k):
        return hx.get(side, lambda value: x_part(value, c, t, k))

    def y_halo(side, c, k):
        return hy.get(side, lambda ref: tile(ref, (c,), 0, k))

    for side, out in ((LOW, y_low), (HIGH, y_high)):
        y_row, t = (0, 0) if side == LOW else (ROWS - 1, nt - 1)
        for k in range(nk):
            w, we, scale = (tile(ref, (side,), 0, k) for ref in (w_y, w_yx, s_y))
            for c in range(3):
                low = moved(x_halo(LOW, c, t, k), y_row, 0)
                high = moved(x_halo(HIGH, c, t, k), y_row, ROWS - 1)
                edge = jnp.where(row == 0, low, high)
                total = tile(acc_y, (side, c), 0, k) + w * y_halo(side, c, k) + we * edge
                own_u = own_side(hy.parity, side, sye, syo, (c,), k)
                put(out, (c,), 0, k, (1.0 - RELAX) * own_u + scale * total)
    for side in (LOW, HIGH):
        x = 0 if side == LOW else nx - 1
        for k in range(nk):
            for t in range(nt):
                w, scale = tile(w_x, (side,), t, k), tile(s_x, (side,), t, k)
                edge_side = LOW if t == 0 else HIGH if t == nt - 1 else None
                for c in range(3):
                    total = tile(acc_x, (side, c), t, k) + w * x_halo(side, c, t, k)
                    if edge_side is not None:
                        y_row = 0 if t == 0 else ROWS - 1
                        total = total + tile(w_xy, (side,), t, k) * moved(y_halo(edge_side, c, k), x, y_row)
                    value = (1.0 - RELAX) * tile(u, (c, x), t, k) + scale * total
                    if side == LOW:
                        put((x_low0, x_low1)[t], (c,), 0, k, value)
                    else:
                        put(x_high, (c,), t, k, value)


def energy_kernel(
    u_in, x_low0, x_low1, y_low, x_high, y_high, material, history_old,
    u, u_out, history, top, half_top, far, half_far, rows, half_rows, sems,
):
    _, nx, ny, nz = u.shape
    nt, nk = ny // ROWS, nz // LANES
    x_low = (x_low0, x_low1)
    insert_faces(
        u,
        lambda side, c, t, k: x_part((x_low, x_high)[side], c, t, k),
        lambda side, c, k: tile((y_low, y_high)[side], (c,), 0, k),
    )
    copies = [pltpu.make_async_copy(u.at[c], u_out.at[c], sems.at[c]) for c in range(3)]
    start_all(copies)

    def body(x, place):
        lane, row = lane_index(), row_index()
        lines = {(c, t): Line(lambda k, c=c, t=t: tile(u, (c, x), t, k), nk) for c in range(3) for t in range(nt)}
        for k in range(nk):
            sums = [None] * nt
            for c in range(3):
                column = [lines[c, t].own(k) for t in range(nt)]
                ya = y_after(column)
                for t in range(nt):
                    v = column[t]
                    b = ya[t] - v
                    if t == nt - 1:
                        b = jnp.where(row == ROWS - 1, 0.0, b)
                    after = lines[c, t].after(k)
                    if k == nk - 1:
                        after = jnp.where(lane == LANES - 1, 0.0, after)
                    d = after - v
                    total = b * b + d * d
                    if place != 1:
                        a = tile(u, (c, x + 1), t, k) - v
                        total = total + a * a
                    sums[t] = total if c == 0 else sums[t] + total
            for t in range(nt):
                half = 0.5 * modulus(tile(material, (x,), t, k))
                if t == nt - 1:
                    put(rows, (x,), 0, k, sums[t])
                    put(half_rows, (x,), 0, k, half)
                if place == 1:
                    put(far, (), t, k, sums[t])
                    put(half_far, (), t, k, half)
                put(history, (x,), t, k, jnp.maximum(tile(history_old, (x,), t, k), half * sums[t]))

    planes_of(nx, body)
    for x in range(nx):
        top[x : x + 1, :] = rows[x, ROWS - 1 : ROWS, :]
        half_top[x : x + 1, :] = half_rows[x, ROWS - 1 : ROWS, :]
    for copy in copies:
        copy.wait()


def last_kernel(
    ids, owners, history_in, top, half_top, far, half_far, x_high, y_high, hy, hx0, hx1, tough_from, damage_from,
    history, history_out, damage_out, energy, damage, tough, sems,
):
    nx, ny, nz = damage.shape
    nt, nk = ny // ROWS, nz // LANES
    count = ids.shape[1]
    hx = (hx0, hx1)
    fetched = [pltpu.make_async_copy(damage_from, damage, sems.at[2])]
    for n in range(count):
        owner = owners[0, n]
        slot = sum([(owners[0, m] == owner).astype(jnp.int32) for m in range(n)], jnp.int32(0))
        fetched.append(pltpu.make_async_copy(tough_from.at[owner, slot], tough.at[n], sems.at[3 + n]))
    start_all(fetched)

    def squares(here, beyond):
        return sum([(beyond(c) - here(c)) ** 2 for c in range(3)])

    for k in range(nk):
        total = tile(top, (), 0, k) + squares(lambda c: tile(y_high, (c,), 0, k), lambda c: tile(hy, (c,), 0, k))
        put(energy, (), 0, k, tile(half_top, (), 0, k) * total)

    def body(x, _):
        for k in range(nk):
            value = jnp.where(row_index() == ROWS - 1, moved(tile(energy, (), 0, k), x, ROWS - 1), 0.0)
            put(history, (x,), nt - 1, k, jnp.maximum(tile(history, (x,), nt - 1, k), value))
        return 0

    lax.fori_loop(0, nx - 1, body, 0)
    for k in range(nk):
        y_term = squares(lambda c: tile(y_high, (c,), 0, k), lambda c: tile(hy, (c,), 0, k))
        for t in range(nt):
            total = tile(far, (), t, k) + squares(lambda c: tile(x_high, (c,), t, k), lambda c: x_part(hx, c, t, k))
            if t == nt - 1:
                total = total + jnp.where(row_index() == ROWS - 1, moved(y_term, nx - 1, ROWS - 1), 0.0)
            put(history, (nx - 1,), t, k, jnp.maximum(tile(history, (nx - 1,), t, k), tile(half_far, (), t, k) * total))
    saved = pltpu.make_async_copy(history, history_out, sems.at[0])
    saved.start()
    for copy in fetched:
        copy.wait()
    per = max(n for n in (1, 2, 3, 4, 6) if count % n == 0)
    cells = [(x, t) for x in range(nx) for t in range(nt)]
    i = lax.broadcasted_iota(jnp.int32, (2 * LANES, LANES), 0) % LANES
    j = lax.broadcasted_iota(jnp.int32, (2 * LANES, LANES), 1)
    beside = (i - j == 1) | (j - i == 1) | ((i == j) & ((i == 0) | (i == LANES - 1)))
    beside = jnp.where(beside, 1.0, 0.0).astype(jnp.bfloat16)

    def z_sums(d):
        whole = jnp.concatenate([d[cell] for cell in cells], axis=0)
        main = whole.astype(jnp.bfloat16)
        rest = (whole - main.astype(F32)).astype(jnp.bfloat16)
        sums = jnp.dot(jnp.concatenate([main, rest], axis=1), beside, preferred_element_type=F32)
        return {cell: sums[n * ROWS : (n + 1) * ROWS] for n, cell in enumerate(cells)}

    def sweep(first, second, d):
        row = row_index()
        sums, new = z_sums(d), {}
        for x in range(nx):
            column = [d[x, t] for t in range(nt)]
            yb, ya = y_before(column), y_after(column)
            yb[0] = jnp.where(row == 0, column[0], yb[0])
            ya[-1] = jnp.where(row == ROWS - 1, column[-1], ya[-1])
            for t in range(nt):
                total = (d[min(x + 1, nx - 1), t] + d[max(x - 1, 0), t]) + (ya[t] + yb[t]) + sums[x, t]
                new[x, t] = first[x, t] + second[x, t] * total
        return new

    def group(q, _):
        states = []
        for p in range(per):
            n = q * per + p
            lanes = pl.ds(pl.multiple_of(ids[0, n] * LANES, LANES), LANES)
            first, second, d = {}, {}, {}
            for x, t in cells:
                part = slice(t * ROWS, (t + 1) * ROWS)
                h2 = 2.0 * history[x, part, lanes]
                g = tough[n, x, part, :]
                g2 = g * LENGTH
                inverse = 1.0 / (g / LENGTH + h2 + 6.0 * g2)
                first[x, t] = h2 * inverse
                second[x, t] = g2 * inverse
                d[x, t] = damage[x, part, lanes]
            states.append((lanes, first, second, d))
        for _ in range(SWEEPS):
            states = [(lanes, first, second, sweep(first, second, d)) for lanes, first, second, d in states]
        for lanes, _, _, d in states:
            for x, t in cells:
                part = slice(t * ROWS, (t + 1) * ROWS)
                damage[x, part, lanes] = jnp.maximum(d[x, t], damage[x, part, lanes])
        return 0

    lax.fori_loop(0, count // per, group, 0)
    done = pltpu.make_async_copy(damage, damage_out, sems.at[1])
    done.start()
    saved.wait()
    done.wait()


def even_pairs(axis):
    size = lax.axis_size(axis)
    pairs = [(i, i + 1) for i in range(0, size - 1, 2)]
    return pairs + [(b, a) for a, b in pairs]


def odd_pairs(axis):
    gx, yz = lax.axis_size("gx"), lax.axis_size("yz")

    def number(place, other):
        return place * yz + other if axis == "gx" else other * yz + place

    size, others = (gx, yz) if axis == "gx" else (yz, gx)
    step = 2 if axis == "gx" else 1
    pairs = [(number(i, o), number(i + 1, o)) for i in range(1, size - 1, 2) for o in range(others)]
    if size % 2 == 0 and others % (2 * step) == 0:
        for end in (0, size - 1):
            pairs += [(number(end, o), number(end, o + step)) for o in range(others) if o % (2 * step) < step]
    return pairs + [(b, a) for a, b in pairs]


def exchange(ye, yo, xe, xo):
    both = ("gx", "yz")
    return (
        lax.ppermute(ye, "yz", even_pairs("yz")),
        lax.ppermute(yo, both, odd_pairs("yz")),
        lax.ppermute(xe, "gx", even_pairs("gx")),
        lax.ppermute(xo, both, odd_pairs("gx")),
    )


def from_above(value, axis):
    size = lax.axis_size(axis)
    return lax.ppermute(value, axis, [(i + 1, i) for i in range(size - 1)])


def call(kernel, outs, ins, scratch=(), aliases=None):
    args, in_specs, out_specs, shapes = [], [], [], []
    for value, space in ins:
        args.append(value if space is pltpu.SMEM else pltpu.with_memory_space_constraint(value, space))
        in_specs.append(pl.BlockSpec(memory_space=space))
    for shape, space in outs:
        shapes.append(space(shape, F32))
        out_specs.append(pl.BlockSpec(memory_space=space))
    return pl.pallas_call(
        kernel,
        out_shape=shapes,
        in_specs=in_specs,
        out_specs=out_specs,
        scratch_shapes=scratch,
        input_output_aliases=aliases or {},
        compiler_params=pltpu.CompilerParams(vmem_limit_bytes=GRANT),
    )(*args)


def here(*shapes):
    return [(shape, VMEM) for shape in shapes]


def kept(*values):
    return [(value, VMEM) for value in values]


def far_off(*values):
    return [(value, HBM) for value in values]


def body(displacement, force, damage, history_old, material, patch_ids, owners, toughness):
    nx, ny, nz = damage.shape
    assert nx == ROWS and ny == 2 * ROWS
    full, cells, halves = (3, nx, ny, nz), (nx, ny, nz), (3, ROWS, nz)

    def faces(count):
        return here(*[(count, nx, nz)] * 2, *[(count, ny, nz)] * 2)

    def copies(count):
        return pltpu.SemaphoreType.DMA((count,))

    arrived = lax.all_to_all(toughness[0], "yz", split_axis=0, concat_axis=0, tiled=True)
    u, stiff, *sent = call(
        begin_kernel,
        here(full, cells) + faces(4),
        far_off(damage, material, displacement),
        [pltpu.VMEM(cells, F32), pltpu.VMEM(cells, jnp.int32), copies(3)],
    )
    brought = exchange(*sent)
    wx, wya, wyb, wza, wzb, scale, u1, acc_x, acc_y, diag_x, diag_y = call(
        inner_one_kernel,
        here((nx - 1, ny, nz), *[cells] * 5, full, (2, 3, ny, nz), (2, 3, nx, nz), (2, ny, nz), (2, 1, nx, nz)),
        kept(u, stiff, force),
        [pltpu.VMEM((2, 3, nx, ROWS, nz), F32), pltpu.VMEM((2, 1, nx, ROWS, nz), F32)],
    )
    *own, w_x, w_xy, s_x, w_y, w_yx, s_y, planes = call(
        face_one_kernel,
        faces(3) + here(*[(2, ny, nz)] * 3, *[(2, nx, nz)] * 3, (2, 3, ny, nz)),
        kept(u, stiff, sent[0], sent[1], acc_x, acc_y, diag_x, diag_y, *brought),
    )
    brought = exchange(*own)
    u1, u2, acc_x, acc_y = call(
        inner_two_kernel,
        here(full, full, (2, 3, ny, nz), (2, 3, nx, nz)),
        kept(u1, scale, force, wx, wya, wyb, wza, wzb, own[0], own[1], planes),
        [pltpu.VMEM((2, 3, nx, ROWS, nz), F32)],
        {0: 0},
    )
    x_low0, x_low1, y_low, x_high, y_high = call(
        face_two_kernel,
        here(halves, halves, (3, nx, nz), (3, ny, nz), (3, nx, nz)),
        kept(u1, own[0], own[1], acc_x, acc_y, w_x, w_xy, s_x, w_y, w_yx, s_y, *brought),
    )
    hy, hx0, hx1 = from_above(y_low, "yz"), from_above(x_low0, "gx"), from_above(x_low1, "gx")
    _, new_displacement, history, *sums = call(
        energy_kernel,
        here(full) + [(full, HBM)] + here(cells, *[(nx, nz)] * 2, *[(ny, nz)] * 2),
        kept(u2, x_low0, x_low1, y_low, x_high, y_high, material, history_old),
        [pltpu.VMEM((nx, ROWS, nz), F32), pltpu.VMEM((nx, ROWS, nz), F32), copies(3)],
        {0: 0},
    )
    count = patch_ids.shape[1]
    _, new_history, new_damage = call(
        last_kernel,
        here(cells) + [(cells, HBM), (cells, HBM)],
        [(patch_ids, pltpu.SMEM), (owners[:, :, 0], pltpu.SMEM)]
        + kept(history, *sums, x_high, y_high, hy, hx0, hx1)
        + far_off(arrived, damage),
        [pltpu.VMEM((nx, nz), F32), pltpu.VMEM(cells, F32), pltpu.VMEM((count,) + arrived.shape[2:], F32), copies(3 + count)],
        {2: 0},
    )
    return (new_displacement, new_history, new_damage)


def solution(mesh):
    return jax.shard_map(
        body,
        mesh=mesh,
        in_specs=(
            P(None, "gx", "yz", None),
            P(None, "gx", "yz", None),
            P("gx", "yz", None),
            P("gx", "yz", None),
            P("gx", "yz", None),
            P(("gx", "yz"), None),
            P(("gx", "yz"), None, None),
            P(("gx", "yz"), None, None, None, None, None),
        ),
        out_specs=(P(None, "gx", "yz", None), P("gx", "yz", None), P("gx", "yz", None)),
        check_vma=False,
    )
```

```python
import jax
import jax.numpy as jnp
from jax import lax
from jax.experimental import pallas as pl
from jax.experimental.pallas import tpu as pltpu
from jax.sharding import PartitionSpec as P

SWEEPS = 8
MODULI = (1.0, 0.5, 4.0, 0.25)
SPRING = 0.05
RELAX = 0.8
LENGTH = 2.0
ROWS = 8
LANES = 128
LOW, HIGH = 0, 1
GRANT = 8 * 1024 * 1024

VMEM = pltpu.MemorySpace.VMEM
HBM = pltpu.MemorySpace.HBM
F32 = jnp.float32


def modulus(material):
    low = jnp.where(material == 0, MODULI[0], MODULI[1])
    high = jnp.where(material == 2, MODULI[2], MODULI[3])
    return jnp.where(material < 2, low, high)


def lane_index():
    return lax.broadcasted_iota(jnp.int32, (ROWS, LANES), 1)


def row_index():
    return lax.broadcasted_iota(jnp.int32, (ROWS, LANES), 0)


def where_tile(lead, t, k):
    return (*lead, slice(t * ROWS, (t + 1) * ROWS), slice(k * LANES, (k + 1) * LANES))


def tile(ref, lead, t, k):
    return ref[where_tile(lead, t, k)]


def put(ref, lead, t, k, value):
    ref[where_tile(lead, t, k)] = value


def moved(value, source, target):
    shift = (target - source) % ROWS if isinstance(source, int) else (target - source + ROWS) % ROWS
    if isinstance(shift, int) and shift == 0:
        return value
    return pltpu.roll(value, shift, 0)


class Line:
    def __init__(self, load, nk):
        self.load, self.nk, self.kept = load, nk, {}

    def get(self, kind, k):
        k = k % self.nk
        if (kind, k) not in self.kept:
            if kind == "own":
                value = self.load(k)
            else:
                value = pltpu.roll(self.get("own", k), LANES - 1 if kind == "next" else 1, 1)
            self.kept[kind, k] = value
        return self.kept[kind, k]

    def own(self, k):
        return self.get("own", k)

    def after(self, k):
        return jnp.where(lane_index() == LANES - 1, self.get("next", k + 1), self.get("next", k))

    def before(self, k):
        return jnp.where(lane_index() == 0, self.get("prev", k - 1), self.get("prev", k))


def y_before(column):
    rolled = [pltpu.roll(v, 1, 0) for v in column]
    row = row_index()
    return rolled[:1] + [jnp.where(row == 0, a, b) for a, b in zip(rolled, rolled[1:])]


def y_after(column):
    rolled = [pltpu.roll(v, ROWS - 1, 0) for v in column]
    row = row_index()
    return [jnp.where(row == ROWS - 1, b, a) for a, b in zip(rolled, rolled[1:])] + rolled[-1:]


def by_parity(parity, even, odd, then):
    @pl.when(parity == 0)
    def _():
        then(odd, even)

    @pl.when(parity == 1)
    def _():
        then(even, odd)


class Halo:
    def __init__(self, axis, even, odd):
        place, size = lax.axis_index(axis), lax.axis_size(axis)
        self.even, self.odd = even, odd
        self.parity = place % 2
        self.inside = (place > 0, place < size - 1)

    def get(self, side, load):
        even, odd = load(self.even), load(self.odd)
        here = self.parity == (1 if side == LOW else 0)
        return jnp.where(self.inside[side], jnp.where(here, even, odd), 0.0)


def planes_of(nx, body):
    body(0, -1)

    def inner(x, _):
        body(x, 0)
        return 0

    lax.fori_loop(1, nx - 1, inner, 0)
    body(nx - 1, 1)


def start_all(copies):
    for copy in copies:
        copy.start()


def pack_planes(even, odd, read, nx, nt):
    def planes(low, high):
        for side, out in ((0, low), (nx - 1, high)):
            for t in range(nt):
                for c in range(out[t].shape[0]):
                    value = read(c, side, t)
                    out[t][c, :, : value.shape[1]] = value

    by_parity(lax.axis_index("gx") % 2, even, odd, planes)


def far_copies(tough, d, far, sems, base):
    me = lax.axis_index("yz")
    return [pltpu.make_async_copy(tough.at[me ^ d ^ p], far.at[p], sems.at[base, p]) for p in (0, 1)]


def begin_kernel(damage, material, field, tough, u, stiff, ye, yo, xe0, xe1, xo0, xo1, far_one, damage_kept, material_kept, sems):
    nx, ny, nz = stiff.shape
    nt = ny // ROWS
    copies = [
        [pltpu.make_async_copy(source.at[x], target.at[x], sems.at[i, x]) for x in range(nx)]
        for i, (source, target) in enumerate(((damage, damage_kept), (material, material_kept)))
    ]
    fields = [pltpu.make_async_copy(field.at[c], u.at[c], sems.at[2, c]) for c in range(3)]
    owed = far_copies(tough, routes(lax.axis_size("yz"))[0], far_one, sems, 3)
    for pair in zip(*copies):
        start_all(pair)
    start_all(fields + owed)
    for x in range(nx):
        copies[0][x].wait()
        copies[1][x].wait()
        d = 1.0 - damage_kept[x]
        stiff[x] = modulus(material_kept[x]) * (d * d + 0.001)
    for copy in fields:
        copy.wait()

    def rows(low, high):
        for side, out in ((0, low), (ny - 1, high)):
            for x in range(nx):
                for c in range(3):
                    out[c, x : x + 1, :] = u[c, x, side : side + 1, :]
                out[3, x : x + 1, :] = stiff[x, side : side + 1, :]

    by_parity(lax.axis_index("yz") % 2, ye, yo, rows)

    def read(c, x, t):
        part = slice(t * ROWS, (t + 1) * ROWS)
        return u[c, x, part, :] if c < 3 else stiff[x, part, :]

    pack_planes((xe0, xe1), (xo0, xo1), read, nx, nt)
    for copy in owed:
        copy.wait()


def relax_inner(x, place, u, load, weights, scale, out, acc_x, acc_y, faces):
    nt, nk = u.shape[2] // ROWS, u.shape[3] // LANES
    lines = {(c, t): Line(lambda k, c=c, t=t: tile(u, (c, x), t, k), nk) for c in range(3) for t in range(nt)}
    for k in range(nk):
        found = [weights(x, t, k) for t in range(nt)]
        scales = [scale(x, t, k) for t in range(nt)]
        for c in range(3):
            column = [lines[c, t].own(k) for t in range(nt)]
            yb, ya = y_before(column), y_after(column)
            for t in range(nt):
                xh, xl, wya, wyb, wza, wzb = found[t]
                total = load(c, x, t, k)
                if place != 1:
                    total = total + xh * tile(u, (c, x + 1), t, k)
                if place != -1:
                    total = total + xl * tile(u, (c, x - 1), t, k)
                total = total + (wya * ya[t] + wyb * yb[t])
                total = total + (wza * lines[c, t].after(k) + wzb * lines[c, t].before(k))
                if place == -1:
                    put(acc_x, (LOW, c), t, k, total)
                if place == 1:
                    put(acc_x, (HIGH, c), t, k, total)
                if t == 0:
                    put(faces, (LOW, c, x), 0, k, total)
                if t == nt - 1:
                    put(faces, (HIGH, c, x), 0, k, total)
                put(out, (c, x), t, k, (1.0 - RELAX) * column[t] + scales[t] * total)


def compact_rows(faces, out, nx):
    for c in range(out.shape[1]):
        for x in range(nx):
            out[LOW, c, x : x + 1, :] = faces[LOW, c, x, 0:1, :]
            out[HIGH, c, x : x + 1, :] = faces[HIGH, c, x, ROWS - 1 : ROWS, :]


def inner_one_kernel(
    u, stiff, force, tough, early0, early1, wx, wya, wyb, wza, wzb, scale, out, acc_x, acc_y, diag_x, diag_y, hop, faces, diag_faces, sems
):
    nx, ny, nz = stiff.shape
    nt, nk = ny // ROWS, nz // LANES
    me = lax.axis_index("yz")
    ways = routes(lax.axis_size("yz"))[1]
    copies = [pltpu.make_async_copy(tough.at[me ^ 1 ^ d], hop.at[i], sems.at[i]) for i, d in enumerate(ways)]
    start_all(copies)

    def prepare(x, place):
        lane, row = lane_index(), row_index()
        lines = [Line(lambda k, t=t: tile(stiff, (x,), t, k), nk) for t in range(nt)]
        for k in range(nk):
            column = [lines[t].own(k) for t in range(nt)]
            yb, ya = y_before(column), y_after(column)
            for t in range(nt):
                s = column[t]
                half = 0.5 * s
                diag = SPRING * s
                if place != 1:
                    w = half + 0.5 * tile(stiff, (x + 1,), t, k)
                    put(wx, (x,), t, k, w)
                    diag = diag + w
                if place != -1:
                    diag = diag + (half + 0.5 * tile(stiff, (x - 1,), t, k))
                w = half + 0.5 * ya[t]
                if t == nt - 1:
                    w = jnp.where(row == ROWS - 1, 0.0, w)
                put(wya, (x,), t, k, w)
                diag = diag + w
                w = half + 0.5 * yb[t]
                if t == 0:
                    w = jnp.where(row == 0, 0.0, w)
                put(wyb, (x,), t, k, w)
                diag = diag + w
                w = half + 0.5 * lines[t].after(k)
                if k == nk - 1:
                    diag = diag + jnp.where(lane == LANES - 1, half, w)
                    w = jnp.where(lane == LANES - 1, 0.0, w)
                else:
                    diag = diag + w
                put(wza, (x,), t, k, w)
                w = half + 0.5 * lines[t].before(k)
                if k == 0:
                    diag = diag + jnp.where(lane == 0, half, w)
                    w = jnp.where(lane == 0, 0.0, w)
                else:
                    diag = diag + w
                put(wzb, (x,), t, k, w)
                put(scale, (x,), t, k, RELAX / diag)
                if place == -1:
                    put(diag_x, (LOW,), t, k, diag)
                if place == 1:
                    put(diag_x, (HIGH,), t, k, diag)
                if t == 0:
                    put(diag_faces, (LOW, 0, x), 0, k, diag)
                if t == nt - 1:
                    put(diag_faces, (HIGH, 0, x), 0, k, diag)

    planes_of(nx, prepare)
    inner_pass(u, force, wx, wya, wyb, wza, wzb, scale, out, acc_x, acc_y, faces)
    compact_rows(diag_faces, diag_y, nx)
    for copy in copies:
        copy.wait()


def inner_pass(u, force, wx, wya, wyb, wza, wzb, scale, out, acc_x, acc_y, faces):
    nx = u.shape[1]

    def body(x, place):
        def weights(x, t, k):
            high = None if place == 1 else tile(wx, (x,), t, k)
            low = None if place == -1 else tile(wx, (x - 1,), t, k)
            return (high, low) + tuple(tile(w, (x,), t, k) for w in (wya, wyb, wza, wzb))

        relax_inner(
            x, place, u, lambda c, x, t, k: tile(force, (c, x), t, k), weights, lambda x, t, k: tile(scale, (x,), t, k), out,
            acc_x, acc_y, faces,
        )

    planes_of(nx, body)
    compact_rows(faces, acc_y, nx)


def x_part(value, c, t, k):
    return tile(value[t], (c,), 0, k) if isinstance(value, tuple) else tile(value, (c,), t, k)


def own_side(parity, side, sent_even, sent_odd, lead, k):
    even, odd = tile(sent_even, lead, 0, k), tile(sent_odd, lead, 0, k)
    return jnp.where(parity == (1 if side == LOW else 0), even, odd)


def face_one_kernel(
    u, stiff, sye, syo, acc_x, acc_y, diag_x, diag_y, hxe0, hye, hyo, hxe1, hxo0, hxo1,
    ye, yo, xe0, xe1, xo0, xo1, w_x, w_xy, s_x, w_y, w_yx, s_y, planes,
):
    _, nx, ny, nz = u.shape
    nt, nk = ny // ROWS, nz // LANES
    hy = Halo("yz", hye, hyo)
    hx = Halo("gx", (hxe0, hxe1), (hxo0, hxo1))
    row = row_index()

    def x_halo(side, c, t, k):
        return hx.get(side, lambda value: x_part(value, c, t, k))

    def y_halo(side, c, k):
        return hy.get(side, lambda ref: tile(ref, (c,), 0, k))

    def y_faces(even, odd):
        for side, out in ((LOW, odd), (HIGH, even)):
            y_row, t = (0, 0) if side == LOW else (ROWS - 1, nt - 1)
            for k in range(nk):
                own = own_side(hy.parity, side, sye, syo, (3,), k)
                w = 0.5 * (own + y_halo(side, 3, k))
                low = moved(x_halo(LOW, 3, t, k), y_row, 0)
                high = moved(x_halo(HIGH, 3, t, k), y_row, ROWS - 1)
                edge = jnp.where(row == 0, low, high)
                we = jnp.where((row == 0) | (row == ROWS - 1), 0.5 * (own + edge), 0.0)
                scale = RELAX / (tile(diag_y, (side, 0), 0, k) + w + we)
                put(w_y, (side,), 0, k, w)
                put(w_yx, (side,), 0, k, we)
                put(s_y, (side,), 0, k, scale)
                for c in range(3):
                    low = moved(x_halo(LOW, c, t, k), y_row, 0)
                    high = moved(x_halo(HIGH, c, t, k), y_row, ROWS - 1)
                    edge = jnp.where(row == 0, low, high)
                    total = tile(acc_y, (side, c), 0, k) + w * y_halo(side, c, k) + we * edge
                    own_u = own_side(hy.parity, side, sye, syo, (c,), k)
                    put(out, (c,), 0, k, (1.0 - RELAX) * own_u + scale * total)

    by_parity(hy.parity, ye, yo, lambda low, high: y_faces(high, low))

    for side in (LOW, HIGH):
            x = 0 if side == LOW else nx - 1
            for k in range(nk):
                for t in range(nt):
                    own = tile(stiff, (x,), t, k)
                    w = 0.5 * (own + x_halo(side, 3, t, k))
                    diag = tile(diag_x, (side,), t, k) + w
                    edge_side = LOW if t == 0 else HIGH if t == nt - 1 else None
                    if edge_side is not None:
                        y_row = 0 if t == 0 else ROWS - 1
                        we = 0.5 * (own + moved(y_halo(edge_side, 3, k), x, y_row))
                        we = jnp.where(row == y_row, we, 0.0)
                        diag = diag + we
                        put(w_xy, (side,), t, k, we)
                    scale = RELAX / diag
                    put(w_x, (side,), t, k, w)
                    put(s_x, (side,), t, k, scale)
                    for c in range(3):
                        total = tile(acc_x, (side, c), t, k) + w * x_halo(side, c, t, k)
                        if edge_side is not None:
                            total = total + we * moved(y_halo(edge_side, c, k), x, y_row)
                        value = (1.0 - RELAX) * tile(u, (c, x), t, k) + scale * total
                        put(planes, (side, c), t, k, value)

    def read(c, x, t):
        return planes[LOW if x == 0 else HIGH, c, t * ROWS : (t + 1) * ROWS, :]

    pack_planes((xe0, xe1), (xo0, xo1), read, nx, nt)


def insert_faces(u, x_face, y_face):
    _, nx, ny, nz = u.shape
    nt, nk = ny // ROWS, nz // LANES
    for side, x in ((LOW, 0), (HIGH, nx - 1)):
        for c in range(3):
            for t in range(nt):
                for k in range(nk):
                    put(u, (c, x), t, k, x_face(side, c, t, k))

    def inner(x, _):
        row = row_index()
        for side, t, place in ((LOW, 0, 0), (HIGH, nt - 1, ROWS - 1)):
            for c in range(3):
                for k in range(nk):
                    value = moved(y_face(side, c, k), x, place)
                    put(u, (c, x), t, k, jnp.where(row == place, value, tile(u, (c, x), t, k)))
        return 0

    lax.fori_loop(1, nx - 1, inner, 0)


def inner_two_kernel(
    u_in, scale, force, wx, wya, wyb, wza, wzb, sye, syo, planes, tough, hop, far_one, early0, early1,
    u, out, acc_x, acc_y, hop_two, *rest,
):
    *fars, faces, sems = rest
    me = lax.axis_index("yz")
    copies = [
        pltpu.make_async_copy(tough.at[me ^ 1], hop_two.at[0], sems.at[2 * len(fars)]),
        pltpu.make_async_copy(far_one.at[1], hop_two.at[1], sems.at[2 * len(fars) + 1]),
    ]
    for i, (d, far) in enumerate(zip(routes(lax.axis_size("yz"))[1], fars)):
        copies.append(pltpu.make_async_copy(tough.at[me ^ d], far.at[0], sems.at[2 * i]))
        copies.append(pltpu.make_async_copy(hop.at[i], far.at[1], sems.at[2 * i + 1]))
    start_all(copies)
    hy = lax.axis_index("yz") % 2
    insert_faces(u, lambda side, c, t, k: tile(planes, (side, c), t, k), lambda side, c, k: own_side(hy, side, sye, syo, (c,), k))
    inner_pass(u, force, wx, wya, wyb, wza, wzb, scale, out, acc_x, acc_y, faces)
    for copy in copies:
        copy.wait()


def face_two_kernel(
    u, sye, syo, acc_x, acc_y, w_x, w_xy, s_x, w_y, w_yx, s_y, hxe0, hye, hyo, hxe1, hxo0, hxo1, *rest
):
    passed = (len(rest) - 5) // 2
    x_low0, x_low1, y_low, x_high, y_high = rest[passed : passed + 5]
    _, nx, ny, nz = u.shape
    nt, nk = ny // ROWS, nz // LANES
    hy = Halo("yz", hye, hyo)
    hx = Halo("gx", (hxe0, hxe1), (hxo0, hxo1))
    row = row_index()

    def x_halo(side, c, t, k):
        return hx.get(side, lambda value: x_part(value, c, t, k))

    def y_halo(side, c, k):
        return hy.get(side, lambda ref: tile(ref, (c,), 0, k))

    for side, out in ((LOW, y_low), (HIGH, y_high)):
        y_row, t = (0, 0) if side == LOW else (ROWS - 1, nt - 1)
        for k in range(nk):
            w, we, scale = (tile(ref, (side,), 0, k) for ref in (w_y, w_yx, s_y))
            for c in range(3):
                low = moved(x_halo(LOW, c, t, k), y_row, 0)
                high = moved(x_halo(HIGH, c, t, k), y_row, ROWS - 1)
                edge = jnp.where(row == 0, low, high)
                total = tile(acc_y, (side, c), 0, k) + w * y_halo(side, c, k) + we * edge
                own_u = own_side(hy.parity, side, sye, syo, (c,), k)
                put(out, (c,), 0, k, (1.0 - RELAX) * own_u + scale * total)
    for side in (LOW, HIGH):
        x = 0 if side == LOW else nx - 1
        for k in range(nk):
            for t in range(nt):
                w, scale = tile(w_x, (side,), t, k), tile(s_x, (side,), t, k)
                edge_side = LOW if t == 0 else HIGH if t == nt - 1 else None
                for c in range(3):
                    total = tile(acc_x, (side, c), t, k) + w * x_halo(side, c, t, k)
                    if edge_side is not None:
                        y_row = 0 if t == 0 else ROWS - 1
                        total = total + tile(w_xy, (side,), t, k) * moved(y_halo(edge_side, c, k), x, y_row)
                    value = (1.0 - RELAX) * tile(u, (c, x), t, k) + scale * total
                    if side == LOW:
                        put((x_low0, x_low1)[t], (c,), 0, k, value)
                    else:
                        put(x_high, (c,), t, k, value)


def energy_kernel(
    u_in, x_low0, x_low1, y_low, x_high, y_high, material, history_old, tough_from, far_one, *rest
):
    *fars, u, u_out, history, top, half_top, far, half_far, tough, rows, half_rows, sems = rest
    _, nx, ny, nz = u.shape
    nt, nk = ny // ROWS, nz // LANES
    x_low = (x_low0, x_low1)
    insert_faces(
        u,
        lambda side, c, t, k: x_part((x_low, x_high)[side], c, t, k),
        lambda side, c, k: tile((y_low, y_high)[side], (c,), 0, k),
    )
    me, size = lax.axis_index("yz"), lax.axis_size("yz")
    first, others = routes(size)
    sources = {0: tough_from.at[me], first: far_one.at[0]}
    for d, arrived in zip(others, fars):
        sources.update({d: arrived.at[0], d ^ 1: arrived.at[1]})
    copies = [pltpu.make_async_copy(u.at[c], u_out.at[c], sems.at[c]) for c in range(3)]
    copies += [pltpu.make_async_copy(source, tough.at[d], sems.at[3 + d]) for d, source in sources.items()]
    start_all(copies)

    def body(x, place):
        lane, row = lane_index(), row_index()
        lines = {(c, t): Line(lambda k, c=c, t=t: tile(u, (c, x), t, k), nk) for c in range(3) for t in range(nt)}
        for k in range(nk):
            sums = [None] * nt
            for c in range(3):
                column = [lines[c, t].own(k) for t in range(nt)]
                ya = y_after(column)
                for t in range(nt):
                    v = column[t]
                    b = ya[t] - v
                    if t == nt - 1:
                        b = jnp.where(row == ROWS - 1, 0.0, b)
                    after = lines[c, t].after(k)
                    if k == nk - 1:
                        after = jnp.where(lane == LANES - 1, 0.0, after)
                    d = after - v
                    total = b * b + d * d
                    if place != 1:
                        a = tile(u, (c, x + 1), t, k) - v
                        total = total + a * a
                    sums[t] = total if c == 0 else sums[t] + total
            for t in range(nt):
                half = 0.5 * modulus(tile(material, (x,), t, k))
                if t == nt - 1:
                    put(rows, (x,), 0, k, sums[t])
                    put(half_rows, (x,), 0, k, half)
                if place == 1:
                    put(far, (), t, k, sums[t])
                    put(half_far, (), t, k, half)
                put(history, (x,), t, k, jnp.maximum(tile(history_old, (x,), t, k), half * sums[t]))

    planes_of(nx, body)
    for x in range(nx):
        top[x : x + 1, :] = rows[x, ROWS - 1 : ROWS, :]
        half_top[x : x + 1, :] = half_rows[x, ROWS - 1 : ROWS, :]
    for copy in copies:
        copy.wait()


def history_kernel(
    history_in, top, half_top, far, half_far, x_high, y_high, hy, hx0, hx1, damage_from, history, damage, energy, sems
):
    nx, ny, nz = damage.shape
    nt, nk = ny // ROWS, nz // LANES
    hx = (hx0, hx1)
    copy = pltpu.make_async_copy(damage_from, damage, sems.at[0])
    copy.start()

    def squares(here, beyond):
        return sum([(beyond(c) - here(c)) ** 2 for c in range(3)])

    for k in range(nk):
        total = tile(top, (), 0, k) + squares(lambda c: tile(y_high, (c,), 0, k), lambda c: tile(hy, (c,), 0, k))
        put(energy, (), 0, k, tile(half_top, (), 0, k) * total)

    def body(x, _):
        for k in range(nk):
            value = jnp.where(row_index() == ROWS - 1, moved(tile(energy, (), 0, k), x, ROWS - 1), 0.0)
            put(history, (x,), nt - 1, k, jnp.maximum(tile(history, (x,), nt - 1, k), value))
        return 0

    lax.fori_loop(0, nx - 1, body, 0)
    for k in range(nk):
        y_term = squares(lambda c: tile(y_high, (c,), 0, k), lambda c: tile(hy, (c,), 0, k))
        for t in range(nt):
            total = tile(far, (), t, k) + squares(lambda c: tile(x_high, (c,), t, k), lambda c: x_part(hx, c, t, k))
            if t == nt - 1:
                total = total + jnp.where(row_index() == ROWS - 1, moved(y_term, nx - 1, ROWS - 1), 0.0)
            put(history, (nx - 1,), t, k, jnp.maximum(tile(history, (nx - 1,), t, k), tile(half_far, (), t, k) * total))
    copy.wait()


def last_kernel(ids, owners, history, damage_in, tough_in, hop_two, damage, tough, history_out, damage_out, sems):
    nx, ny, nz = damage.shape
    nt = ny // ROWS
    count = ids.shape[1]
    me, size = lax.axis_index("yz"), lax.axis_size("yz")
    fetched = [pltpu.make_async_copy(hop_two.at[i], tough.at[d ^ 1], sems.at[2 + i]) for i, d in enumerate((0, routes(size)[0]))]
    start_all(fetched)
    saved = pltpu.make_async_copy(history, history_out, sems.at[0])
    saved.start()
    for copy in fetched:
        copy.wait()
    per = max(n for n in (1, 2, 3, 4, 6) if count % n == 0)
    cells = [(x, t) for x in range(nx) for t in range(nt)]
    i = lax.broadcasted_iota(jnp.int32, (2 * LANES, LANES), 0) % LANES
    j = lax.broadcasted_iota(jnp.int32, (2 * LANES, LANES), 1)
    beside = (i - j == 1) | (j - i == 1) | ((i == j) & ((i == 0) | (i == LANES - 1)))
    beside = jnp.where(beside, 1.0, 0.0).astype(jnp.bfloat16)

    def z_sums(d):
        whole = jnp.concatenate([d[cell] for cell in cells], axis=0)
        main = whole.astype(jnp.bfloat16)
        rest = (whole - main.astype(F32)).astype(jnp.bfloat16)
        sums = jnp.dot(jnp.concatenate([main, rest], axis=1), beside, preferred_element_type=F32)
        return {cell: sums[n * ROWS : (n + 1) * ROWS] for n, cell in enumerate(cells)}

    def sweep(first, second, d):
        row = row_index()
        sums, new = z_sums(d), {}
        for x in range(nx):
            column = [d[x, t] for t in range(nt)]
            yb, ya = y_before(column), y_after(column)
            yb[0] = jnp.where(row == 0, column[0], yb[0])
            ya[-1] = jnp.where(row == ROWS - 1, column[-1], ya[-1])
            for t in range(nt):
                total = (d[min(x + 1, nx - 1), t] + d[max(x - 1, 0), t]) + (ya[t] + yb[t]) + sums[x, t]
                new[x, t] = first[x, t] + second[x, t] * total
        return new

    def group(q, _):
        states = []
        for p in range(per):
            n = q * per + p
            owner = owners[0, n]
            slot = lax.fori_loop(0, n, lambda m, found: found + (owners[0, m] == owner).astype(jnp.int32), jnp.int32(0))
            lanes = pl.ds(pl.multiple_of(ids[0, n] * LANES, LANES), LANES)
            first, second, d = {}, {}, {}
            for x, t in cells:
                part = slice(t * ROWS, (t + 1) * ROWS)
                h2 = 2.0 * history[x, part, lanes]
                g = tough[owner ^ me, slot, x, part, :]
                g2 = g * LENGTH
                inverse = 1.0 / (g / LENGTH + h2 + 6.0 * g2)
                first[x, t] = h2 * inverse
                second[x, t] = g2 * inverse
                d[x, t] = damage[x, part, lanes]
            states.append((lanes, first, second, d))
        for _ in range(SWEEPS):
            states = [(lanes, first, second, sweep(first, second, d)) for lanes, first, second, d in states]
        for lanes, _, _, d in states:
            for x, t in cells:
                part = slice(t * ROWS, (t + 1) * ROWS)
                damage[x, part, lanes] = jnp.maximum(d[x, t], damage[x, part, lanes])
        return 0

    lax.fori_loop(0, count // per, group, 0)
    done = pltpu.make_async_copy(damage, damage_out, sems.at[1])
    done.start()
    saved.wait()
    done.wait()


def even_pairs(axis):
    size = lax.axis_size(axis)
    pairs = [(i, i + 1) for i in range(0, size - 1, 2)]
    return pairs + [(b, a) for a, b in pairs]


def odd_pairs(axis):
    gx, yz = lax.axis_size("gx"), lax.axis_size("yz")

    def number(place, other):
        return place * yz + other if axis == "gx" else other * yz + place

    size, others = (gx, yz) if axis == "gx" else (yz, gx)
    step = 2 if axis == "gx" else 1
    pairs = [(number(i, o), number(i + 1, o)) for i in range(1, size - 1, 2) for o in range(others)]
    if size % 2 == 0 and others % (2 * step) == 0:
        for end in (0, size - 1):
            pairs += [(number(end, o), number(end, o + step)) for o in range(others) if o % (2 * step) < step]
    return pairs + [(b, a) for a, b in pairs]


def exchange(ye, yo, xe0, xe1, xo0, xo1):
    both = ("gx", "yz")
    return (
        lax.ppermute(xe0, "gx", even_pairs("gx")),
        lax.ppermute(ye, "yz", even_pairs("yz")),
        lax.ppermute(yo, both, odd_pairs("yz")),
        lax.ppermute(xe1, "gx", even_pairs("gx")),
        lax.ppermute(xo0, both, odd_pairs("gx")),
        lax.ppermute(xo1, both, odd_pairs("gx")),
    )


def routes(size):
    assert size >= 8 and size & (size - 1) == 0
    return 4, tuple(d for d in (6, 2) + tuple(range(8, size, 2)))


def across(value, d):
    return lax.ppermute(value, "yz", [(i, i ^ d) for i in range(lax.axis_size("yz"))])


def from_above(value, axis):
    size = lax.axis_size(axis)
    return lax.ppermute(value, axis, [(i + 1, i) for i in range(size - 1)])


def call(kernel, outs, ins, scratch=(), aliases=None):
    args, in_specs, out_specs, shapes = [], [], [], []
    for value, space in ins:
        args.append(value if space is pltpu.SMEM else pltpu.with_memory_space_constraint(value, space))
        in_specs.append(pl.BlockSpec(memory_space=space))
    for shape, space in outs:
        shapes.append(space(shape, F32))
        out_specs.append(pl.BlockSpec(memory_space=space))
    return pl.pallas_call(
        kernel,
        out_shape=shapes,
        in_specs=in_specs,
        out_specs=out_specs,
        scratch_shapes=scratch,
        input_output_aliases=aliases or {},
        compiler_params=pltpu.CompilerParams(vmem_limit_bytes=GRANT),
    )(*args)


def here(*shapes):
    return [(shape, VMEM) for shape in shapes]


def kept(*values):
    return [(value, VMEM) for value in values]


def far_off(*values):
    return [(value, HBM) for value in values]


def body(displacement, force, damage, history_old, material, patch_ids, owners, toughness):
    nx, ny, nz = damage.shape
    assert nx == ROWS and ny == 2 * ROWS
    full, cells, halves = (3, nx, ny, nz), (nx, ny, nz), (3, ROWS, nz)

    def faces(count):
        return here(*[(count, nx, nz)] * 2, *[(count, ROWS, nz)] * 2, *[(count, ROWS, nz + LANES)] * 2)

    def copies(count):
        return pltpu.SemaphoreType.DMA((count,))

    tough = toughness[0]
    pair = (2,) + tough.shape[1:]
    first, others = routes(lax.axis_size("yz"))
    u, stiff, *sent, far_one = call(
        begin_kernel,
        here(full, cells) + faces(4) + here(pair),
        far_off(damage, material, displacement, tough),
        [pltpu.VMEM(cells, F32), pltpu.VMEM(cells, jnp.int32), pltpu.SemaphoreType.DMA((4, nx))],
    )
    brought = exchange(*sent)
    far_one = across(far_one, first)
    wx, wya, wyb, wza, wzb, scale, u1, acc_x, acc_y, diag_x, diag_y, hop = call(
        inner_one_kernel,
        here((nx - 1, ny, nz), *[cells] * 5, full, (2, 3, ny, nz), (2, 3, nx, nz), (2, ny, nz), (2, 1, nx, nz))
        + here((len(others),) + tough.shape[1:]),
        kept(u, stiff, force) + far_off(tough) + kept(brought[0], brought[3]),
        [pltpu.VMEM((2, 3, nx, ROWS, nz), F32), pltpu.VMEM((2, 1, nx, ROWS, nz), F32), copies(len(others))],
    )
    hop = across(hop, 1)
    *own, w_x, w_xy, s_x, w_y, w_yx, s_y, planes = call(
        face_one_kernel,
        faces(3) + here(*[(2, ny, nz)] * 3, *[(2, nx, nz)] * 3, (2, 3, ny, nz)),
        kept(u, stiff, sent[0], sent[1], acc_x, acc_y, diag_x, diag_y, *brought),
    )
    brought = exchange(*own)
    u1, u2, acc_x, acc_y, hop_two, *fars = call(
        inner_two_kernel,
        here(full, full, (2, 3, ny, nz), (2, 3, nx, nz), pair, *[pair for _ in others]),
        kept(u1, scale, force, wx, wya, wyb, wza, wzb, own[0], own[1], planes)
        + far_off(tough)
        + kept(hop, far_one, brought[0], brought[3]),
        [pltpu.VMEM((2, 3, nx, ROWS, nz), F32), copies(2 + 2 * len(others))],
        {0: 0},
    )
    lasts = [across(value, d) for d, value in zip(others, fars)]
    x_low0, x_low1, y_low, x_high, y_high, hop_two = call(
        face_two_kernel,
        here(halves, halves, (3, nx, nz), (3, ny, nz), (3, nx, nz), hop_two.shape),
        kept(u1, own[0], own[1], acc_x, acc_y, w_x, w_xy, s_x, w_y, w_yx, s_y, *brought, hop_two),
        (),
        {17: 5},
    )
    hop_two = across(hop_two, 1)
    hy, hx0, hx1 = from_above(y_low, "yz"), from_above(x_low0, "gx"), from_above(x_low1, "gx")
    _, new_displacement, history, *sums, tough_kept = call(
        energy_kernel,
        here(full) + [(full, HBM)] + here(cells, *[(nx, nz)] * 2, *[(ny, nz)] * 2, tough.shape),
        kept(u2, x_low0, x_low1, y_low, x_high, y_high, material, history_old) + far_off(tough) + kept(far_one, *lasts),
        [pltpu.VMEM((nx, ROWS, nz), F32), pltpu.VMEM((nx, ROWS, nz), F32), copies(3 + tough.shape[0])],
        {0: 0},
    )
    history, damage_kept = call(
        history_kernel,
        here(cells, cells),
        kept(history, *sums, x_high, y_high, hy, hx0, hx1) + far_off(damage),
        [pltpu.VMEM((nx, nz), F32), copies(1)],
        {0: 0},
    )
    _, _, new_history, new_damage = call(
        last_kernel,
        here(cells, tough.shape) + [(cells, HBM), (cells, HBM)],
        [(patch_ids, pltpu.SMEM), (owners[:, :, 0], pltpu.SMEM)] + kept(history, damage_kept, tough_kept, hop_two),
        [copies(4)],
        {3: 0, 4: 1},
    )
    return (new_displacement, new_history, new_damage)


def solution(mesh):
    return jax.shard_map(
        body,
        mesh=mesh,
        in_specs=(
            P(None, "gx", "yz", None),
            P(None, "gx", "yz", None),
            P("gx", "yz", None),
            P("gx", "yz", None),
            P("gx", "yz", None),
            P(("gx", "yz"), None),
            P(("gx", "yz"), None, None),
            P(("gx", "yz"), None, None, None, None, None),
        ),
        out_specs=(P(None, "gx", "yz", None), P("gx", "yz", None), P("gx", "yz", None)),
        check_vma=False,
    )
```

```python
import jax
import jax.numpy as jnp
from jax import lax
from jax.experimental import pallas as pl
from jax.experimental.pallas import tpu as pltpu
from jax.sharding import PartitionSpec as P

SWEEPS = 8
MODULI = (1.0, 0.5, 4.0, 0.25)
SPRING = 0.05
RELAX = 0.8
LENGTH = 2.0
ROWS = 8
LANES = 128
LOW, HIGH = 0, 1
GRANT = 8 * 1024 * 1024

VMEM = pltpu.MemorySpace.VMEM
HBM = pltpu.MemorySpace.HBM
F32 = jnp.float32


def modulus(material):
    low = jnp.where(material == 0, MODULI[0], MODULI[1])
    high = jnp.where(material == 2, MODULI[2], MODULI[3])
    return jnp.where(material < 2, low, high)


def lane_index():
    return lax.broadcasted_iota(jnp.int32, (ROWS, LANES), 1)


def row_index():
    return lax.broadcasted_iota(jnp.int32, (ROWS, LANES), 0)


def where_tile(lead, t, k):
    return (*lead, slice(t * ROWS, (t + 1) * ROWS), slice(k * LANES, (k + 1) * LANES))


def tile(ref, lead, t, k):
    return ref[where_tile(lead, t, k)]


def put(ref, lead, t, k, value):
    ref[where_tile(lead, t, k)] = value


def moved(value, source, target):
    shift = (target - source) % ROWS if isinstance(source, int) else (target - source + ROWS) % ROWS
    if isinstance(shift, int) and shift == 0:
        return value
    return pltpu.roll(value, shift, 0)


class Line:
    def __init__(self, load, nk):
        self.load, self.nk, self.kept = load, nk, {}

    def get(self, kind, k):
        k = k % self.nk
        if (kind, k) not in self.kept:
            if kind == "own":
                value = self.load(k)
            else:
                value = pltpu.roll(self.get("own", k), LANES - 1 if kind == "next" else 1, 1)
            self.kept[kind, k] = value
        return self.kept[kind, k]

    def own(self, k):
        return self.get("own", k)

    def after(self, k):
        return jnp.where(lane_index() == LANES - 1, self.get("next", k + 1), self.get("next", k))

    def before(self, k):
        return jnp.where(lane_index() == 0, self.get("prev", k - 1), self.get("prev", k))


def y_before(column):
    rolled = [pltpu.roll(v, 1, 0) for v in column]
    row = row_index()
    return rolled[:1] + [jnp.where(row == 0, a, b) for a, b in zip(rolled, rolled[1:])]


def y_after(column):
    rolled = [pltpu.roll(v, ROWS - 1, 0) for v in column]
    row = row_index()
    return [jnp.where(row == ROWS - 1, b, a) for a, b in zip(rolled, rolled[1:])] + rolled[-1:]


def by_parity(parity, even, odd, then):
    @pl.when(parity == 0)
    def _():
        then(odd, even)

    @pl.when(parity == 1)
    def _():
        then(even, odd)


class Halo:
    def __init__(self, axis, even, odd):
        place, size = lax.axis_index(axis), lax.axis_size(axis)
        self.even, self.odd = even, odd
        self.parity = place % 2
        self.inside = (place > 0, place < size - 1)

    def get(self, side, load):
        even, odd = load(self.even), load(self.odd)
        here = self.parity == (1 if side == LOW else 0)
        return jnp.where(self.inside[side], jnp.where(here, even, odd), 0.0)


def planes_of(nx, body):
    body(0, -1)

    def inner(x, _):
        body(x, 0)
        return 0

    lax.fori_loop(1, nx - 1, inner, 0)
    body(nx - 1, 1)


def start_all(copies):
    for copy in copies:
        copy.start()


def pack_planes(even, odd, read, nt, nx, components):
    def planes(low, high):
        for side, out in ((0, low), (nx - 1, high)):
            for t in range(nt):
                for c in components:
                    value = read(c, side, t)
                    out[t][c, :, : value.shape[1]] = value

    by_parity(lax.axis_index("gx") % 2, even, odd, planes)


def far_copies(tough, d, far, sems, base):
    me = lax.axis_index("yz")
    return [pltpu.make_async_copy(tough.at[me ^ d ^ p], far.at[p], sems.at[base, p]) for p in (0, 1)]


def begin_kernel(damage, material, field, tough, u, stiff, ye, yo, xe0, xe1, xo0, xo1, far_one, damage_kept, material_kept, sems):
    nx, ny, nz = stiff.shape
    nt = ny // ROWS
    copies = [
        [pltpu.make_async_copy(source.at[x], target.at[x], sems.at[i, x]) for x in range(nx)]
        for i, (source, target) in enumerate(((damage, damage_kept), (material, material_kept)))
    ]
    fields = [pltpu.make_async_copy(field.at[c], u.at[c], sems.at[2, c]) for c in range(3)]
    owed = far_copies(tough, routes(lax.axis_size("yz"))[0], far_one, sems, 3)
    start_all(fields)
    for pair in zip(*copies):
        start_all(pair)
    start_all(owed)
    y_parity = lax.axis_index("yz") % 2
    for copy in fields:
        copy.wait()

    def u_rows(low, high):
        for side, out in ((0, low), (ny - 1, high)):
            for x in range(nx):
                for c in range(3):
                    out[c, x : x + 1, :] = u[c, x, side : side + 1, :]

    def stiff_rows(low, high):
        for side, out in ((0, low), (ny - 1, high)):
            for x in range(nx):
                out[3, x : x + 1, :] = stiff[x, side : side + 1, :]

    by_parity(y_parity, ye, yo, u_rows)
    pack_planes((xe0, xe1), (xo0, xo1), lambda c, x, t: u[c, x, t * ROWS : (t + 1) * ROWS, :], nt, nx, range(3))
    for x in range(nx):
        copies[0][x].wait()
        copies[1][x].wait()
        d = 1.0 - damage_kept[x]
        stiff[x] = modulus(material_kept[x]) * (d * d + 0.001)
    by_parity(y_parity, ye, yo, stiff_rows)
    pack_planes((xe0, xe1), (xo0, xo1), lambda c, x, t: stiff[x, t * ROWS : (t + 1) * ROWS, :], nt, nx, (3,))
    for copy in owed:
        copy.wait()


def relax_inner(x, place, u, load, weights, scale, out, acc_x, acc_y, faces):
    nt, nk = u.shape[2] // ROWS, u.shape[3] // LANES
    lines = {(c, t): Line(lambda k, c=c, t=t: tile(u, (c, x), t, k), nk) for c in range(3) for t in range(nt)}
    for k in range(nk):
        found = [weights(x, t, k) for t in range(nt)]
        scales = [scale(x, t, k) for t in range(nt)]
        for c in range(3):
            column = [lines[c, t].own(k) for t in range(nt)]
            yb, ya = y_before(column), y_after(column)
            for t in range(nt):
                xh, xl, wya, wyb, wza, wzb = found[t]
                total = load(c, x, t, k)
                if place != 1:
                    total = total + xh * tile(u, (c, x + 1), t, k)
                if place != -1:
                    total = total + xl * tile(u, (c, x - 1), t, k)
                total = total + (wya * ya[t] + wyb * yb[t])
                total = total + (wza * lines[c, t].after(k) + wzb * lines[c, t].before(k))
                if place == -1:
                    put(acc_x, (LOW, c), t, k, total)
                if place == 1:
                    put(acc_x, (HIGH, c), t, k, total)
                if t == 0:
                    put(faces, (LOW, c, x), 0, k, total)
                if t == nt - 1:
                    put(faces, (HIGH, c, x), 0, k, total)
                put(out, (c, x), t, k, (1.0 - RELAX) * column[t] + scales[t] * total)


def compact_rows(faces, out, nx):
    for c in range(out.shape[1]):
        for x in range(nx):
            out[LOW, c, x : x + 1, :] = faces[LOW, c, x, 0:1, :]
            out[HIGH, c, x : x + 1, :] = faces[HIGH, c, x, ROWS - 1 : ROWS, :]


def inner_one_kernel(
    u, stiff, force, tough, early0, early1, wx, wya, wyb, wza, wzb, scale, out, acc_x, acc_y, diag_x, diag_y, hop, faces, diag_faces, sems
):
    nx, ny, nz = stiff.shape
    nt, nk = ny // ROWS, nz // LANES
    me = lax.axis_index("yz")
    ways = routes(lax.axis_size("yz"))[1]
    copies = [pltpu.make_async_copy(tough.at[me ^ 1 ^ d], hop.at[i], sems.at[i]) for i, d in enumerate(ways)]
    start_all(copies)

    def prepare(x, place):
        lane, row = lane_index(), row_index()
        lines = [Line(lambda k, t=t: tile(stiff, (x,), t, k), nk) for t in range(nt)]
        for k in range(nk):
            column = [lines[t].own(k) for t in range(nt)]
            yb, ya = y_before(column), y_after(column)
            for t in range(nt):
                s = column[t]
                half = 0.5 * s
                diag = SPRING * s
                if place != 1:
                    w = half + 0.5 * tile(stiff, (x + 1,), t, k)
                    put(wx, (x,), t, k, w)
                    diag = diag + w
                if place != -1:
                    diag = diag + (half + 0.5 * tile(stiff, (x - 1,), t, k))
                w = half + 0.5 * ya[t]
                if t == nt - 1:
                    w = jnp.where(row == ROWS - 1, 0.0, w)
                put(wya, (x,), t, k, w)
                diag = diag + w
                w = half + 0.5 * yb[t]
                if t == 0:
                    w = jnp.where(row == 0, 0.0, w)
                put(wyb, (x,), t, k, w)
                diag = diag + w
                w = half + 0.5 * lines[t].after(k)
                if k == nk - 1:
                    diag = diag + jnp.where(lane == LANES - 1, half, w)
                    w = jnp.where(lane == LANES - 1, 0.0, w)
                else:
                    diag = diag + w
                put(wza, (x,), t, k, w)
                w = half + 0.5 * lines[t].before(k)
                if k == 0:
                    diag = diag + jnp.where(lane == 0, half, w)
                    w = jnp.where(lane == 0, 0.0, w)
                else:
                    diag = diag + w
                put(wzb, (x,), t, k, w)
                put(scale, (x,), t, k, RELAX / diag)
                if place == -1:
                    put(diag_x, (LOW,), t, k, diag)
                if place == 1:
                    put(diag_x, (HIGH,), t, k, diag)
                if t == 0:
                    put(diag_faces, (LOW, 0, x), 0, k, diag)
                if t == nt - 1:
                    put(diag_faces, (HIGH, 0, x), 0, k, diag)

    planes_of(nx, prepare)
    inner_pass(u, force, wx, wya, wyb, wza, wzb, scale, out, acc_x, acc_y, faces)
    compact_rows(diag_faces, diag_y, nx)
    for copy in copies:
        copy.wait()


def inner_pass(u, force, wx, wya, wyb, wza, wzb, scale, out, acc_x, acc_y, faces):
    nx = u.shape[1]

    def body(x, place):
        def weights(x, t, k):
            high = None if place == 1 else tile(wx, (x,), t, k)
            low = None if place == -1 else tile(wx, (x - 1,), t, k)
            return (high, low) + tuple(tile(w, (x,), t, k) for w in (wya, wyb, wza, wzb))

        relax_inner(
            x, place, u, lambda c, x, t, k: tile(force, (c, x), t, k), weights, lambda x, t, k: tile(scale, (x,), t, k), out,
            acc_x, acc_y, faces,
        )

    planes_of(nx, body)
    compact_rows(faces, acc_y, nx)


def x_part(value, c, t, k):
    return tile(value[t], (c,), 0, k) if isinstance(value, tuple) else tile(value, (c,), t, k)


def own_side(parity, side, sent_even, sent_odd, lead, k):
    even, odd = tile(sent_even, lead, 0, k), tile(sent_odd, lead, 0, k)
    return jnp.where(parity == (1 if side == LOW else 0), even, odd)


def face_one_kernel(
    u, stiff, sye, syo, acc_x, acc_y, diag_x, diag_y, hxe0, hye, hyo, hxe1, hxo0, hxo1, hop_in,
    ye, yo, xe0, xe1, xo0, xo1, w_x, w_xy, s_x, w_y, w_yx, s_y, planes, hop,
):
    _, nx, ny, nz = u.shape
    nt, nk = ny // ROWS, nz // LANES
    hy = Halo("yz", hye, hyo)
    hx = Halo("gx", (hxe0, hxe1), (hxo0, hxo1))
    row = row_index()

    def x_halo(side, c, t, k):
        return hx.get(side, lambda value: x_part(value, c, t, k))

    def y_halo(side, c, k):
        return hy.get(side, lambda ref: tile(ref, (c,), 0, k))

    def y_faces(even, odd):
        for side, out in ((LOW, odd), (HIGH, even)):
            y_row, t = (0, 0) if side == LOW else (ROWS - 1, nt - 1)
            for k in range(nk):
                own = own_side(hy.parity, side, sye, syo, (3,), k)
                w = 0.5 * (own + y_halo(side, 3, k))
                low = moved(x_halo(LOW, 3, t, k), y_row, 0)
                high = moved(x_halo(HIGH, 3, t, k), y_row, ROWS - 1)
                edge = jnp.where(row == 0, low, high)
                we = jnp.where((row == 0) | (row == ROWS - 1), 0.5 * (own + edge), 0.0)
                scale = RELAX / (tile(diag_y, (side, 0), 0, k) + w + we)
                put(w_y, (side,), 0, k, w)
                put(w_yx, (side,), 0, k, we)
                put(s_y, (side,), 0, k, scale)
                for c in range(3):
                    low = moved(x_halo(LOW, c, t, k), y_row, 0)
                    high = moved(x_halo(HIGH, c, t, k), y_row, ROWS - 1)
                    edge = jnp.where(row == 0, low, high)
                    total = tile(acc_y, (side, c), 0, k) + w * y_halo(side, c, k) + we * edge
                    own_u = own_side(hy.parity, side, sye, syo, (c,), k)
                    put(out, (c,), 0, k, (1.0 - RELAX) * own_u + scale * total)

    by_parity(hy.parity, ye, yo, lambda low, high: y_faces(high, low))

    for side in (LOW, HIGH):
            x = 0 if side == LOW else nx - 1
            for k in range(nk):
                for t in range(nt):
                    own = tile(stiff, (x,), t, k)
                    w = 0.5 * (own + x_halo(side, 3, t, k))
                    diag = tile(diag_x, (side,), t, k) + w
                    edge_side = LOW if t == 0 else HIGH if t == nt - 1 else None
                    if edge_side is not None:
                        y_row = 0 if t == 0 else ROWS - 1
                        we = 0.5 * (own + moved(y_halo(edge_side, 3, k), x, y_row))
                        we = jnp.where(row == y_row, we, 0.0)
                        diag = diag + we
                        put(w_xy, (side,), t, k, we)
                    scale = RELAX / diag
                    put(w_x, (side,), t, k, w)
                    put(s_x, (side,), t, k, scale)
                    for c in range(3):
                        total = tile(acc_x, (side, c), t, k) + w * x_halo(side, c, t, k)
                        if edge_side is not None:
                            total = total + we * moved(y_halo(edge_side, c, k), x, y_row)
                        value = (1.0 - RELAX) * tile(u, (c, x), t, k) + scale * total
                        put(planes, (side, c), t, k, value)

    def read(c, x, t):
        return planes[LOW if x == 0 else HIGH, c, t * ROWS : (t + 1) * ROWS, :]

    pack_planes((xe0, xe1), (xo0, xo1), read, nt, nx, range(3))


def insert_faces(u, x_face, y_face):
    _, nx, ny, nz = u.shape
    nt, nk = ny // ROWS, nz // LANES
    for side, x in ((LOW, 0), (HIGH, nx - 1)):
        for c in range(3):
            for t in range(nt):
                for k in range(nk):
                    put(u, (c, x), t, k, x_face(side, c, t, k))

    def inner(x, _):
        row = row_index()
        for side, t, place in ((LOW, 0, 0), (HIGH, nt - 1, ROWS - 1)):
            for c in range(3):
                for k in range(nk):
                    value = moved(y_face(side, c, k), x, place)
                    put(u, (c, x), t, k, jnp.where(row == place, value, tile(u, (c, x), t, k)))
        return 0

    lax.fori_loop(1, nx - 1, inner, 0)


def inner_two_kernel(
    u_in, scale, force, wx, wya, wyb, wza, wzb, sye, syo, planes, tough, hop, far_one, early0, early1,
    u, out, acc_x, acc_y, hop_two, *rest,
):
    *fars, faces, sems = rest
    me = lax.axis_index("yz")
    copies = [
        pltpu.make_async_copy(tough.at[me ^ 1], hop_two.at[0], sems.at[2 * len(fars)]),
        pltpu.make_async_copy(far_one.at[1], hop_two.at[1], sems.at[2 * len(fars) + 1]),
    ]
    for i, (d, far) in enumerate(zip(routes(lax.axis_size("yz"))[1], fars)):
        copies.append(pltpu.make_async_copy(tough.at[me ^ d], far.at[0], sems.at[2 * i]))
        copies.append(pltpu.make_async_copy(hop.at[i], far.at[1], sems.at[2 * i + 1]))
    start_all(copies)
    hy = lax.axis_index("yz") % 2
    insert_faces(u, lambda side, c, t, k: tile(planes, (side, c), t, k), lambda side, c, k: own_side(hy, side, sye, syo, (c,), k))
    inner_pass(u, force, wx, wya, wyb, wza, wzb, scale, out, acc_x, acc_y, faces)
    for copy in copies:
        copy.wait()


def face_two_kernel(
    u, sye, syo, acc_x, acc_y, w_x, w_xy, s_x, w_y, w_yx, s_y, hxe0, hye, hyo, hxe1, hxo0, hxo1, *rest
):
    passed = (len(rest) - 5) // 2
    x_low0, x_low1, y_low, x_high, y_high = rest[passed : passed + 5]
    _, nx, ny, nz = u.shape
    nt, nk = ny // ROWS, nz // LANES
    hy = Halo("yz", hye, hyo)
    hx = Halo("gx", (hxe0, hxe1), (hxo0, hxo1))
    row = row_index()

    def x_halo(side, c, t, k):
        return hx.get(side, lambda value: x_part(value, c, t, k))

    def y_halo(side, c, k):
        return hy.get(side, lambda ref: tile(ref, (c,), 0, k))

    for side, out in ((LOW, y_low), (HIGH, y_high)):
        y_row, t = (0, 0) if side == LOW else (ROWS - 1, nt - 1)
        for k in range(nk):
            w, we, scale = (tile(ref, (side,), 0, k) for ref in (w_y, w_yx, s_y))
            for c in range(3):
                low = moved(x_halo(LOW, c, t, k), y_row, 0)
                high = moved(x_halo(HIGH, c, t, k), y_row, ROWS - 1)
                edge = jnp.where(row == 0, low, high)
                total = tile(acc_y, (side, c), 0, k) + w * y_halo(side, c, k) + we * edge
                own_u = own_side(hy.parity, side, sye, syo, (c,), k)
                put(out, (c,), 0, k, (1.0 - RELAX) * own_u + scale * total)
    for side in (LOW, HIGH):
        x = 0 if side == LOW else nx - 1
        for k in range(nk):
            for t in range(nt):
                w, scale = tile(w_x, (side,), t, k), tile(s_x, (side,), t, k)
                edge_side = LOW if t == 0 else HIGH if t == nt - 1 else None
                for c in range(3):
                    total = tile(acc_x, (side, c), t, k) + w * x_halo(side, c, t, k)
                    if edge_side is not None:
                        y_row = 0 if t == 0 else ROWS - 1
                        total = total + tile(w_xy, (side,), t, k) * moved(y_halo(edge_side, c, k), x, y_row)
                    value = (1.0 - RELAX) * tile(u, (c, x), t, k) + scale * total
                    if side == LOW:
                        put((x_low0, x_low1)[t], (c,), 0, k, value)
                    else:
                        put(x_high, (c,), t, k, value)


def energy_kernel(
    u_in, x_low0, x_low1, y_low, x_high, y_high, material, history_old, tough_from, damage_from, far_one, *rest
):
    *fars, u, u_out, history, top, half_top, far, half_far, tough, damage, rows, half_rows, sems = rest
    _, nx, ny, nz = u.shape
    nt, nk = ny // ROWS, nz // LANES
    x_low = (x_low0, x_low1)
    insert_faces(
        u,
        lambda side, c, t, k: x_part((x_low, x_high)[side], c, t, k),
        lambda side, c, k: tile((y_low, y_high)[side], (c,), 0, k),
    )
    me, size = lax.axis_index("yz"), lax.axis_size("yz")
    first, others = routes(size)
    sources = {0: tough_from.at[me], first: far_one.at[0]}
    for d, arrived in zip(others, fars):
        sources.update({d: arrived.at[0], d ^ 1: arrived.at[1]})
    copies = [pltpu.make_async_copy(u.at[c], u_out.at[c], sems.at[c]) for c in range(3)]
    copies += [pltpu.make_async_copy(source, tough.at[d], sems.at[4 + d]) for d, source in sources.items()]
    copies.append(pltpu.make_async_copy(damage_from, damage, sems.at[3]))
    start_all(copies)

    def body(x, place):
        lane, row = lane_index(), row_index()
        lines = {(c, t): Line(lambda k, c=c, t=t: tile(u, (c, x), t, k), nk) for c in range(3) for t in range(nt)}
        for k in range(nk):
            sums = [None] * nt
            for c in range(3):
                column = [lines[c, t].own(k) for t in range(nt)]
                ya = y_after(column)
                for t in range(nt):
                    v = column[t]
                    b = ya[t] - v
                    if t == nt - 1:
                        b = jnp.where(row == ROWS - 1, 0.0, b)
                    after = lines[c, t].after(k)
                    if k == nk - 1:
                        after = jnp.where(lane == LANES - 1, 0.0, after)
                    d = after - v
                    total = b * b + d * d
                    if place != 1:
                        a = tile(u, (c, x + 1), t, k) - v
                        total = total + a * a
                    sums[t] = total if c == 0 else sums[t] + total
            for t in range(nt):
                half = 0.5 * modulus(tile(material, (x,), t, k))
                if t == nt - 1:
                    put(rows, (x,), 0, k, sums[t])
                    put(half_rows, (x,), 0, k, half)
                if place == 1:
                    put(far, (), t, k, sums[t])
                    put(half_far, (), t, k, half)
                put(history, (x,), t, k, jnp.maximum(tile(history_old, (x,), t, k), half * sums[t]))

    planes_of(nx, body)
    for x in range(nx):
        top[x : x + 1, :] = rows[x, ROWS - 1 : ROWS, :]
        half_top[x : x + 1, :] = half_rows[x, ROWS - 1 : ROWS, :]
    for copy in copies:
        copy.wait()


def history_kernel(
    history_in, top, half_top, far, half_far, x_high, y_high, hy, hx0, hx1, history, energy
):
    nx, ny, nz = history.shape
    nt, nk = ny // ROWS, nz // LANES
    hx = (hx0, hx1)

    def squares(here, beyond):
        return sum([(beyond(c) - here(c)) ** 2 for c in range(3)])

    for k in range(nk):
        total = tile(top, (), 0, k) + squares(lambda c: tile(y_high, (c,), 0, k), lambda c: tile(hy, (c,), 0, k))
        put(energy, (), 0, k, tile(half_top, (), 0, k) * total)

    def body(x, _):
        for k in range(nk):
            value = jnp.where(row_index() == ROWS - 1, moved(tile(energy, (), 0, k), x, ROWS - 1), 0.0)
            put(history, (x,), nt - 1, k, jnp.maximum(tile(history, (x,), nt - 1, k), value))
        return 0

    lax.fori_loop(0, nx - 1, body, 0)
    for k in range(nk):
        y_term = squares(lambda c: tile(y_high, (c,), 0, k), lambda c: tile(hy, (c,), 0, k))
        for t in range(nt):
            total = tile(far, (), t, k) + squares(lambda c: tile(x_high, (c,), t, k), lambda c: x_part(hx, c, t, k))
            if t == nt - 1:
                total = total + jnp.where(row_index() == ROWS - 1, moved(y_term, nx - 1, ROWS - 1), 0.0)
            put(history, (nx - 1,), t, k, jnp.maximum(tile(history, (nx - 1,), t, k), tile(half_far, (), t, k) * total))


def last_kernel(ids, owners, history, damage, tough, hop_two, history_out, damage_out, result, sems):
    nx, ny, nz = damage.shape
    nt = ny // ROWS
    count = ids.shape[1]
    me, size = lax.axis_index("yz"), lax.axis_size("yz")
    late = routes(size)[0] ^ 1
    saved = pltpu.make_async_copy(history, history_out, sems.at[0])
    saved.start()
    rest = pltpu.make_async_copy(damage, damage_out, sems.at[1])
    rest.start()
    finished = []
    per = max(n for n in (1, 2, 3, 4, 6) if count % n == 0)
    cells = [(x, t) for x in range(nx) for t in range(nt)]
    i = lax.broadcasted_iota(jnp.int32, (2 * LANES, LANES), 0) % LANES
    j = lax.broadcasted_iota(jnp.int32, (2 * LANES, LANES), 1)
    beside = (i - j == 1) | (j - i == 1) | ((i == j) & ((i == 0) | (i == LANES - 1)))
    beside = jnp.where(beside, 1.0, 0.0).astype(jnp.bfloat16)

    def z_sums(d):
        whole = jnp.concatenate([d[cell] for cell in cells], axis=0)
        main = whole.astype(jnp.bfloat16)
        rest = (whole - main.astype(F32)).astype(jnp.bfloat16)
        sums = jnp.dot(jnp.concatenate([main, rest], axis=1), beside, preferred_element_type=F32)
        return {cell: sums[n * ROWS : (n + 1) * ROWS] for n, cell in enumerate(cells)}

    def sweep(first, second, d):
        row = row_index()
        sums, new = z_sums(d), {}
        for x in range(nx):
            column = [d[x, t] for t in range(nt)]
            yb, ya = y_before(column), y_after(column)
            yb[0] = jnp.where(row == 0, column[0], yb[0])
            ya[-1] = jnp.where(row == ROWS - 1, column[-1], ya[-1])
            for t in range(nt):
                total = (d[min(x + 1, nx - 1), t] + d[max(x - 1, 0), t]) + (ya[t] + yb[t]) + sums[x, t]
                new[x, t] = first[x, t] + second[x, t] * total
        return new

    def group(q):
        states = []
        for p in range(per):
            n = q * per + p
            owner = owners[0, n]
            slot = sum([(owners[0, m] == owner).astype(jnp.int32) for m in range(n)], jnp.int32(0))
            lanes = pl.ds(pl.multiple_of(ids[0, n] * LANES, LANES), LANES)
            which = (owner ^ me == late).astype(jnp.int32)
            by_hop = (owner ^ me == 1) | (owner ^ me == late)
            first, second, d = {}, {}, {}
            for x, t in cells:
                part = slice(t * ROWS, (t + 1) * ROWS)
                h2 = 2.0 * history[x, part, lanes]
                g = tough[owner ^ me, slot, x, part, :]
                g = jnp.where(by_hop, hop_two[which, slot, x, part, :], g)
                g2 = g * LENGTH
                inverse = 1.0 / (g / LENGTH + h2 + 6.0 * g2)
                first[x, t] = h2 * inverse
                second[x, t] = g2 * inverse
                d[x, t] = damage[x, part, lanes]
            states.append((n, lanes, first, second, d))
        for _ in range(SWEEPS):
            states = [(n, lanes, first, second, sweep(first, second, d)) for n, lanes, first, second, d in states]
        if q == 0:
            rest.wait()
        for n, lanes, _, _, d in states:
            for x, t in cells:
                part = slice(t * ROWS, (t + 1) * ROWS)
                result[n, x, part, :] = jnp.maximum(d[x, t], damage[x, part, lanes])
            finished.append(pltpu.make_async_copy(result.at[n], damage_out.at[:, :, lanes], sems.at[2 + n]))
            finished[-1].start()

    for q in range(count // per):
        group(q)
    for copy in [saved] + finished:
        copy.wait()


def even_pairs(axis):
    size = lax.axis_size(axis)
    pairs = [(i, i + 1) for i in range(0, size - 1, 2)]
    return pairs + [(b, a) for a, b in pairs]


def odd_pairs(axis):
    gx, yz = lax.axis_size("gx"), lax.axis_size("yz")

    def number(place, other):
        return place * yz + other if axis == "gx" else other * yz + place

    size, others = (gx, yz) if axis == "gx" else (yz, gx)
    step = 2 if axis == "gx" else 1
    pairs = [(number(i, o), number(i + 1, o)) for i in range(1, size - 1, 2) for o in range(others)]
    if size % 2 == 0 and others % (2 * step) == 0:
        for end in (0, size - 1):
            pairs += [(number(end, o), number(end, o + step)) for o in range(others) if o % (2 * step) < step]
    return pairs + [(b, a) for a, b in pairs]


def exchange(ye, yo, xe0, xe1, xo0, xo1):
    both = ("gx", "yz")
    return (
        lax.ppermute(xe0, "gx", even_pairs("gx")),
        lax.ppermute(ye, "yz", even_pairs("yz")),
        lax.ppermute(yo, both, odd_pairs("yz")),
        lax.ppermute(xe1, "gx", even_pairs("gx")),
        lax.ppermute(xo0, both, odd_pairs("gx")),
        lax.ppermute(xo1, both, odd_pairs("gx")),
    )


def routes(size):
    assert size >= 8 and size & (size - 1) == 0
    return 4, tuple(d for d in (6, 2) + tuple(range(8, size, 2)))


def across(value, d):
    return lax.ppermute(value, "yz", [(i, i ^ d) for i in range(lax.axis_size("yz"))])


def from_above(value, axis):
    size = lax.axis_size(axis)
    return lax.ppermute(value, axis, [(i + 1, i) for i in range(size - 1)])


def call(kernel, outs, ins, scratch=(), aliases=None):
    args, in_specs, out_specs, shapes = [], [], [], []
    for value, space in ins:
        args.append(value if space is pltpu.SMEM else pltpu.with_memory_space_constraint(value, space))
        in_specs.append(pl.BlockSpec(memory_space=space))
    for shape, space in outs:
        shapes.append(space(shape, F32))
        out_specs.append(pl.BlockSpec(memory_space=space))
    return pl.pallas_call(
        kernel,
        out_shape=shapes,
        in_specs=in_specs,
        out_specs=out_specs,
        scratch_shapes=scratch,
        input_output_aliases=aliases or {},
        compiler_params=pltpu.CompilerParams(vmem_limit_bytes=GRANT),
    )(*args)


def here(*shapes):
    return [(shape, VMEM) for shape in shapes]


def kept(*values):
    return [(value, VMEM) for value in values]


def far_off(*values):
    return [(value, HBM) for value in values]


def body(displacement, force, damage, history_old, material, patch_ids, owners, toughness):
    nx, ny, nz = damage.shape
    assert nx == ROWS and ny == 2 * ROWS
    full, cells, halves = (3, nx, ny, nz), (nx, ny, nz), (3, ROWS, nz)

    def faces(count):
        return here(*[(count, nx, nz)] * 2, *[(count, ROWS, nz)] * 2, *[(count, ROWS, nz + LANES)] * 2)

    def copies(count):
        return pltpu.SemaphoreType.DMA((count,))

    tough = toughness[0]
    pair = (2,) + tough.shape[1:]
    first, others = routes(lax.axis_size("yz"))
    u, stiff, *sent, far_one = call(
        begin_kernel,
        here(full, cells) + faces(4) + here(pair),
        far_off(damage, material, displacement, tough),
        [pltpu.VMEM(cells, F32), pltpu.VMEM(cells, jnp.int32), pltpu.SemaphoreType.DMA((4, nx))],
    )
    brought = exchange(*sent)
    far_one = across(far_one, first)
    wx, wya, wyb, wza, wzb, scale, u1, acc_x, acc_y, diag_x, diag_y, hop = call(
        inner_one_kernel,
        here((nx - 1, ny, nz), *[cells] * 5, full, (2, 3, ny, nz), (2, 3, nx, nz), (2, ny, nz), (2, 1, nx, nz))
        + here((len(others),) + tough.shape[1:]),
        kept(u, stiff, force) + far_off(tough) + kept(brought[0], brought[3]),
        [pltpu.VMEM((2, 3, nx, ROWS, nz), F32), pltpu.VMEM((2, 1, nx, ROWS, nz), F32), copies(len(others))],
    )
    *own, w_x, w_xy, s_x, w_y, w_yx, s_y, planes, hop = call(
        face_one_kernel,
        faces(3) + here(*[(2, ny, nz)] * 3, *[(2, nx, nz)] * 3, (2, 3, ny, nz), hop.shape),
        kept(u, stiff, sent[0], sent[1], acc_x, acc_y, diag_x, diag_y, *brought, hop),
        (),
        {14: 13},
    )
    hop = across(hop, 1)
    brought = exchange(*own)
    u1, u2, acc_x, acc_y, hop_two, *fars = call(
        inner_two_kernel,
        here(full, full, (2, 3, ny, nz), (2, 3, nx, nz), pair, *[pair for _ in others]),
        kept(u1, scale, force, wx, wya, wyb, wza, wzb, own[0], own[1], planes)
        + far_off(tough)
        + kept(hop, far_one, brought[0], brought[3]),
        [pltpu.VMEM((2, 3, nx, ROWS, nz), F32), copies(2 + 2 * len(others))],
        {0: 0},
    )
    lasts = [across(value, d) for d, value in zip(others, fars)]
    x_low0, x_low1, y_low, x_high, y_high, hop_two = call(
        face_two_kernel,
        here(halves, halves, (3, nx, nz), (3, ny, nz), (3, nx, nz), hop_two.shape),
        kept(u1, own[0], own[1], acc_x, acc_y, w_x, w_xy, s_x, w_y, w_yx, s_y, *brought, hop_two),
        (),
        {17: 5},
    )
    hop_two = across(hop_two, 1)
    hy, hx0, hx1 = from_above(y_low, "yz"), from_above(x_low0, "gx"), from_above(x_low1, "gx")
    _, new_displacement, history, *sums, tough_kept, damage_kept = call(
        energy_kernel,
        here(full) + [(full, HBM)] + here(cells, *[(nx, nz)] * 2, *[(ny, nz)] * 2, tough.shape, cells),
        kept(u2, x_low0, x_low1, y_low, x_high, y_high, material, history_old) + far_off(tough, damage)
        + kept(far_one, *lasts),
        [pltpu.VMEM((nx, ROWS, nz), F32), pltpu.VMEM((nx, ROWS, nz), F32), copies(4 + tough.shape[0])],
        {0: 0},
    )
    (history,) = call(
        history_kernel,
        here(cells),
        kept(history, *sums, x_high, y_high, hy, hx0, hx1),
        [pltpu.VMEM((nx, nz), F32)],
        {0: 0},
    )
    count = patch_ids.shape[1]
    new_history, new_damage = call(
        last_kernel,
        [(cells, HBM), (cells, HBM)],
        [(patch_ids, pltpu.SMEM), (owners[:, :, 0], pltpu.SMEM)] + kept(history, damage_kept, tough_kept, hop_two),
        [pltpu.VMEM((count, nx, ny, LANES), F32), copies(2 + count)],
    )
    return (new_displacement, new_history, new_damage)


def solution(mesh):
    return jax.shard_map(
        body,
        mesh=mesh,
        in_specs=(
            P(None, "gx", "yz", None),
            P(None, "gx", "yz", None),
            P("gx", "yz", None),
            P("gx", "yz", None),
            P("gx", "yz", None),
            P(("gx", "yz"), None),
            P(("gx", "yz"), None, None),
            P(("gx", "yz"), None, None, None, None, None),
        ),
        out_specs=(P(None, "gx", "yz", None), P("gx", "yz", None), P("gx", "yz", None)),
        check_vma=False,
    )
```

```python
import jax
import jax.numpy as jnp
from jax import lax
from jax.experimental import pallas as pl
from jax.experimental.pallas import tpu as pltpu
from jax.sharding import PartitionSpec as P

SWEEPS = 8
MODULI = (1.0, 0.5, 4.0, 0.25)
SPRING = 0.05
RELAX = 0.8
LENGTH = 2.0
ROWS = 8
LANES = 128
LOW, HIGH = 0, 1
GRANT = 8 * 1024 * 1024

VMEM = pltpu.MemorySpace.VMEM
HBM = pltpu.MemorySpace.HBM
F32 = jnp.float32


def modulus(material):
    low = jnp.where(material == 0, MODULI[0], MODULI[1])
    high = jnp.where(material == 2, MODULI[2], MODULI[3])
    return jnp.where(material < 2, low, high)


def lane_index():
    return lax.broadcasted_iota(jnp.int32, (ROWS, LANES), 1)


def row_index():
    return lax.broadcasted_iota(jnp.int32, (ROWS, LANES), 0)


def where_tile(lead, t, k):
    return (*lead, slice(t * ROWS, (t + 1) * ROWS), slice(k * LANES, (k + 1) * LANES))


def tile(ref, lead, t, k):
    return ref[where_tile(lead, t, k)]


def put(ref, lead, t, k, value):
    ref[where_tile(lead, t, k)] = value


def moved(value, source, target):
    shift = (target - source) % ROWS if isinstance(source, int) else (target - source + ROWS) % ROWS
    if isinstance(shift, int) and shift == 0:
        return value
    return pltpu.roll(value, shift, 0)


class Line:
    def __init__(self, load, nk):
        self.load, self.nk, self.kept = load, nk, {}

    def get(self, kind, k):
        k = k % self.nk
        if (kind, k) not in self.kept:
            if kind == "own":
                value = self.load(k)
            else:
                value = pltpu.roll(self.get("own", k), LANES - 1 if kind == "next" else 1, 1)
            self.kept[kind, k] = value
        return self.kept[kind, k]

    def own(self, k):
        return self.get("own", k)

    def after(self, k):
        return jnp.where(lane_index() == LANES - 1, self.get("next", k + 1), self.get("next", k))

    def before(self, k):
        return jnp.where(lane_index() == 0, self.get("prev", k - 1), self.get("prev", k))


def y_before(column):
    rolled = [pltpu.roll(v, 1, 0) for v in column]
    row = row_index()
    return rolled[:1] + [jnp.where(row == 0, a, b) for a, b in zip(rolled, rolled[1:])]


def y_after(column):
    rolled = [pltpu.roll(v, ROWS - 1, 0) for v in column]
    row = row_index()
    return [jnp.where(row == ROWS - 1, b, a) for a, b in zip(rolled, rolled[1:])] + rolled[-1:]


def by_parity(parity, even, odd, then):
    @pl.when(parity == 0)
    def _():
        then(odd, even)

    @pl.when(parity == 1)
    def _():
        then(even, odd)


class Halo:
    def __init__(self, axis, even, odd):
        place, size = lax.axis_index(axis), lax.axis_size(axis)
        self.even, self.odd = even, odd
        self.parity = place % 2
        self.inside = (place > 0, place < size - 1)

    def get(self, side, load):
        even, odd = load(self.even), load(self.odd)
        here = self.parity == (1 if side == LOW else 0)
        return jnp.where(self.inside[side], jnp.where(here, even, odd), 0.0)


def planes_of(nx, body):
    body(0, -1)

    def inner(x, _):
        body(x, 0)
        return 0

    lax.fori_loop(1, nx - 1, inner, 0)
    body(nx - 1, 1)


def start_all(copies):
    for copy in copies:
        copy.start()


def pack_planes(even, odd, read, nt, nx, components):
    def planes(low, high):
        for side, out in ((0, low), (nx - 1, high)):
            for t in range(nt):
                for c in components:
                    value = read(c, side, t)
                    out[t][c, :, : value.shape[1]] = value

    by_parity(lax.axis_index("gx") % 2, even, odd, planes)


def far_copies(tough, d, far, sems, base):
    me = lax.axis_index("yz")
    return [pltpu.make_async_copy(tough.at[me ^ d ^ p], far.at[p], sems.at[base, p]) for p in (0, 1)]


def begin_kernel(damage, material, field, tough, u, stiff, ye, yo, xe0, xe1, xo0, xo1, far_one, damage_kept, material_kept, sems):
    nx, ny, nz = stiff.shape
    nt = ny // ROWS
    copies = [
        [pltpu.make_async_copy(source.at[x], target.at[x], sems.at[i, x]) for x in range(nx)]
        for i, (source, target) in enumerate(((damage, damage_kept), (material, material_kept)))
    ]
    fields = [pltpu.make_async_copy(field.at[c], u.at[c], sems.at[2, c]) for c in range(3)]
    owed = far_copies(tough, routes(lax.axis_size("yz"))[0], far_one, sems, 3)
    start_all(fields)
    for pair in zip(*copies):
        start_all(pair)
    start_all(owed)
    y_parity = lax.axis_index("yz") % 2
    for copy in fields:
        copy.wait()

    def u_rows(low, high):
        for side, out in ((0, low), (ny - 1, high)):
            for x in range(nx):
                for c in range(3):
                    out[c, x : x + 1, :] = u[c, x, side : side + 1, :]

    def stiff_rows(low, high):
        for side, out in ((0, low), (ny - 1, high)):
            for x in range(nx):
                out[3, x : x + 1, :] = stiff[x, side : side + 1, :]

    by_parity(y_parity, ye, yo, u_rows)
    pack_planes((xe0, xe1), (xo0, xo1), lambda c, x, t: u[c, x, t * ROWS : (t + 1) * ROWS, :], nt, nx, range(3))
    for x in range(nx):
        copies[0][x].wait()
        copies[1][x].wait()
        d = 1.0 - damage_kept[x]
        stiff[x] = modulus(material_kept[x]) * (d * d + 0.001)
    by_parity(y_parity, ye, yo, stiff_rows)
    pack_planes((xe0, xe1), (xo0, xo1), lambda c, x, t: stiff[x, t * ROWS : (t + 1) * ROWS, :], nt, nx, (3,))
    for copy in owed:
        copy.wait()


def relax_inner(x, place, u, load, weights, scale, out, acc_x, acc_y, faces):
    nt, nk = u.shape[2] // ROWS, u.shape[3] // LANES
    lines = {(c, t): Line(lambda k, c=c, t=t: tile(u, (c, x), t, k), nk) for c in range(3) for t in range(nt)}
    for k in range(nk):
        found = [weights(x, t, k) for t in range(nt)]
        scales = [scale(x, t, k) for t in range(nt)]
        for c in range(3):
            column = [lines[c, t].own(k) for t in range(nt)]
            yb, ya = y_before(column), y_after(column)
            for t in range(nt):
                xh, xl, wya, wyb, wza, wzb = found[t]
                total = load(c, x, t, k)
                if place != 1:
                    total = total + xh * tile(u, (c, x + 1), t, k)
                if place != -1:
                    total = total + xl * tile(u, (c, x - 1), t, k)
                total = total + (wya * ya[t] + wyb * yb[t])
                total = total + (wza * lines[c, t].after(k) + wzb * lines[c, t].before(k))
                if place == -1:
                    put(acc_x, (LOW, c), t, k, total)
                if place == 1:
                    put(acc_x, (HIGH, c), t, k, total)
                if t == 0:
                    put(faces, (LOW, c, x), 0, k, total)
                if t == nt - 1:
                    put(faces, (HIGH, c, x), 0, k, total)
                put(out, (c, x), t, k, (1.0 - RELAX) * column[t] + scales[t] * total)


def compact_rows(faces, out, nx):
    for c in range(out.shape[1]):
        for x in range(nx):
            out[LOW, c, x : x + 1, :] = faces[LOW, c, x, 0:1, :]
            out[HIGH, c, x : x + 1, :] = faces[HIGH, c, x, ROWS - 1 : ROWS, :]


def inner_one_kernel(
    u, stiff, force, tough, early0, early1, wx, wya, wyb, wza, wzb, scale, out, acc_x, acc_y, diag_x, diag_y, hop, faces, diag_faces, sems
):
    nx, ny, nz = stiff.shape
    nt, nk = ny // ROWS, nz // LANES
    me = lax.axis_index("yz")
    ways = routes(lax.axis_size("yz"))[1]
    copies = [pltpu.make_async_copy(tough.at[me ^ 1 ^ d], hop.at[i], sems.at[i]) for i, d in enumerate(ways)]
    start_all(copies)

    def prepare(x, place):
        lane, row = lane_index(), row_index()
        lines = [Line(lambda k, t=t: tile(stiff, (x,), t, k), nk) for t in range(nt)]
        for k in range(nk):
            column = [lines[t].own(k) for t in range(nt)]
            yb, ya = y_before(column), y_after(column)
            for t in range(nt):
                s = column[t]
                half = 0.5 * s
                diag = SPRING * s
                if place != 1:
                    w = half + 0.5 * tile(stiff, (x + 1,), t, k)
                    put(wx, (x,), t, k, w)
                    diag = diag + w
                if place != -1:
                    diag = diag + (half + 0.5 * tile(stiff, (x - 1,), t, k))
                w = half + 0.5 * ya[t]
                if t == nt - 1:
                    w = jnp.where(row == ROWS - 1, 0.0, w)
                put(wya, (x,), t, k, w)
                diag = diag + w
                w = half + 0.5 * yb[t]
                if t == 0:
                    w = jnp.where(row == 0, 0.0, w)
                put(wyb, (x,), t, k, w)
                diag = diag + w
                w = half + 0.5 * lines[t].after(k)
                if k == nk - 1:
                    diag = diag + jnp.where(lane == LANES - 1, half, w)
                    w = jnp.where(lane == LANES - 1, 0.0, w)
                else:
                    diag = diag + w
                put(wza, (x,), t, k, w)
                w = half + 0.5 * lines[t].before(k)
                if k == 0:
                    diag = diag + jnp.where(lane == 0, half, w)
                    w = jnp.where(lane == 0, 0.0, w)
                else:
                    diag = diag + w
                put(wzb, (x,), t, k, w)
                put(scale, (x,), t, k, RELAX / diag)
                if place == -1:
                    put(diag_x, (LOW,), t, k, diag)
                if place == 1:
                    put(diag_x, (HIGH,), t, k, diag)
                if t == 0:
                    put(diag_faces, (LOW, 0, x), 0, k, diag)
                if t == nt - 1:
                    put(diag_faces, (HIGH, 0, x), 0, k, diag)

    planes_of(nx, prepare)
    inner_pass(u, force, wx, wya, wyb, wza, wzb, scale, out, acc_x, acc_y, faces)
    compact_rows(diag_faces, diag_y, nx)
    for copy in copies:
        copy.wait()


def inner_pass(u, force, wx, wya, wyb, wza, wzb, scale, out, acc_x, acc_y, faces):
    nx = u.shape[1]

    def body(x, place):
        def weights(x, t, k):
            high = None if place == 1 else tile(wx, (x,), t, k)
            low = None if place == -1 else tile(wx, (x - 1,), t, k)
            return (high, low) + tuple(tile(w, (x,), t, k) for w in (wya, wyb, wza, wzb))

        relax_inner(
            x, place, u, lambda c, x, t, k: tile(force, (c, x), t, k), weights, lambda x, t, k: tile(scale, (x,), t, k), out,
            acc_x, acc_y, faces,
        )

    planes_of(nx, body)
    compact_rows(faces, acc_y, nx)


def x_part(value, c, t, k):
    return tile(value[t], (c,), 0, k) if isinstance(value, tuple) else tile(value, (c,), t, k)


def own_side(parity, side, sent_even, sent_odd, lead, k):
    even, odd = tile(sent_even, lead, 0, k), tile(sent_odd, lead, 0, k)
    return jnp.where(parity == (1 if side == LOW else 0), even, odd)


def face_one_kernel(
    u, stiff, sye, syo, acc_x, acc_y, diag_x, diag_y, hxe0, hye, hyo, hxe1, hxo0, hxo1, hop_in,
    ye, yo, xe0, xe1, xo0, xo1, w_x, w_xy, s_x, w_y, w_yx, s_y, planes, hop,
):
    _, nx, ny, nz = u.shape
    nt, nk = ny // ROWS, nz // LANES
    hy = Halo("yz", hye, hyo)
    hx = Halo("gx", (hxe0, hxe1), (hxo0, hxo1))
    row = row_index()

    def x_halo(side, c, t, k):
        return hx.get(side, lambda value: x_part(value, c, t, k))

    def y_halo(side, c, k):
        return hy.get(side, lambda ref: tile(ref, (c,), 0, k))

    def y_faces(even, odd):
        for side, out in ((LOW, odd), (HIGH, even)):
            y_row, t = (0, 0) if side == LOW else (ROWS - 1, nt - 1)
            for k in range(nk):
                own = own_side(hy.parity, side, sye, syo, (3,), k)
                w = 0.5 * (own + y_halo(side, 3, k))
                low = moved(x_halo(LOW, 3, t, k), y_row, 0)
                high = moved(x_halo(HIGH, 3, t, k), y_row, ROWS - 1)
                edge = jnp.where(row == 0, low, high)
                we = jnp.where((row == 0) | (row == ROWS - 1), 0.5 * (own + edge), 0.0)
                scale = RELAX / (tile(diag_y, (side, 0), 0, k) + w + we)
                put(w_y, (side,), 0, k, w)
                put(w_yx, (side,), 0, k, we)
                put(s_y, (side,), 0, k, scale)
                for c in range(3):
                    low = moved(x_halo(LOW, c, t, k), y_row, 0)
                    high = moved(x_halo(HIGH, c, t, k), y_row, ROWS - 1)
                    edge = jnp.where(row == 0, low, high)
                    total = tile(acc_y, (side, c), 0, k) + w * y_halo(side, c, k) + we * edge
                    own_u = own_side(hy.parity, side, sye, syo, (c,), k)
                    put(out, (c,), 0, k, (1.0 - RELAX) * own_u + scale * total)

    by_parity(hy.parity, ye, yo, lambda low, high: y_faces(high, low))

    for side in (LOW, HIGH):
            x = 0 if side == LOW else nx - 1
            for k in range(nk):
                for t in range(nt):
                    own = tile(stiff, (x,), t, k)
                    w = 0.5 * (own + x_halo(side, 3, t, k))
                    diag = tile(diag_x, (side,), t, k) + w
                    edge_side = LOW if t == 0 else HIGH if t == nt - 1 else None
                    if edge_side is not None:
                        y_row = 0 if t == 0 else ROWS - 1
                        we = 0.5 * (own + moved(y_halo(edge_side, 3, k), x, y_row))
                        we = jnp.where(row == y_row, we, 0.0)
                        diag = diag + we
                        put(w_xy, (side,), t, k, we)
                    scale = RELAX / diag
                    put(w_x, (side,), t, k, w)
                    put(s_x, (side,), t, k, scale)
                    for c in range(3):
                        total = tile(acc_x, (side, c), t, k) + w * x_halo(side, c, t, k)
                        if edge_side is not None:
                            total = total + we * moved(y_halo(edge_side, c, k), x, y_row)
                        value = (1.0 - RELAX) * tile(u, (c, x), t, k) + scale * total
                        put(planes, (side, c), t, k, value)

    def read(c, x, t):
        return planes[LOW if x == 0 else HIGH, c, t * ROWS : (t + 1) * ROWS, :]

    pack_planes((xe0, xe1), (xo0, xo1), read, nt, nx, range(3))


def insert_faces(u, x_face, y_face):
    _, nx, ny, nz = u.shape
    nt, nk = ny // ROWS, nz // LANES
    for side, x in ((LOW, 0), (HIGH, nx - 1)):
        for c in range(3):
            for t in range(nt):
                for k in range(nk):
                    put(u, (c, x), t, k, x_face(side, c, t, k))

    def inner(x, _):
        row = row_index()
        for side, t, place in ((LOW, 0, 0), (HIGH, nt - 1, ROWS - 1)):
            for c in range(3):
                for k in range(nk):
                    value = moved(y_face(side, c, k), x, place)
                    put(u, (c, x), t, k, jnp.where(row == place, value, tile(u, (c, x), t, k)))
        return 0

    lax.fori_loop(1, nx - 1, inner, 0)


def inner_two_kernel(
    u_in, scale, force, wx, wya, wyb, wza, wzb, sye, syo, planes, tough, far_one, early0, early1,
    u, out, acc_x, acc_y, hop_two, *rest,
):
    *fars, faces, sems = rest
    me = lax.axis_index("yz")
    copies = [
        pltpu.make_async_copy(tough.at[me ^ 1], hop_two.at[0], sems.at[len(fars)]),
        pltpu.make_async_copy(far_one.at[1], hop_two.at[1], sems.at[len(fars) + 1]),
    ]
    for i, (d, far) in enumerate(zip(routes(lax.axis_size("yz"))[1], fars)):
        copies.append(pltpu.make_async_copy(tough.at[me ^ d], far.at[0], sems.at[i]))
    start_all(copies)
    hy = lax.axis_index("yz") % 2
    insert_faces(u, lambda side, c, t, k: tile(planes, (side, c), t, k), lambda side, c, k: own_side(hy, side, sye, syo, (c,), k))
    inner_pass(u, force, wx, wya, wyb, wza, wzb, scale, out, acc_x, acc_y, faces)
    for copy in copies:
        copy.wait()


def forward_kernel(hop, *rest):
    for i, far in enumerate(rest[len(rest) // 2 :]):
        far[1] = hop[i]


def face_two_kernel(
    u, sye, syo, acc_x, acc_y, w_x, w_xy, s_x, w_y, w_yx, s_y, hxe0, hye, hyo, hxe1, hxo0, hxo1, *rest
):
    passed = (len(rest) - 5) // 2
    x_low0, x_low1, y_low, x_high, y_high = rest[passed : passed + 5]
    _, nx, ny, nz = u.shape
    nt, nk = ny // ROWS, nz // LANES
    hy = Halo("yz", hye, hyo)
    hx = Halo("gx", (hxe0, hxe1), (hxo0, hxo1))
    row = row_index()

    def x_halo(side, c, t, k):
        return hx.get(side, lambda value: x_part(value, c, t, k))

    def y_halo(side, c, k):
        return hy.get(side, lambda ref: tile(ref, (c,), 0, k))

    for side, out in ((LOW, y_low), (HIGH, y_high)):
        y_row, t = (0, 0) if side == LOW else (ROWS - 1, nt - 1)
        for k in range(nk):
            w, we, scale = (tile(ref, (side,), 0, k) for ref in (w_y, w_yx, s_y))
            for c in range(3):
                low = moved(x_halo(LOW, c, t, k), y_row, 0)
                high = moved(x_halo(HIGH, c, t, k), y_row, ROWS - 1)
                edge = jnp.where(row == 0, low, high)
                total = tile(acc_y, (side, c), 0, k) + w * y_halo(side, c, k) + we * edge
                own_u = own_side(hy.parity, side, sye, syo, (c,), k)
                put(out, (c,), 0, k, (1.0 - RELAX) * own_u + scale * total)
    for side in (LOW, HIGH):
        x = 0 if side == LOW else nx - 1
        for k in range(nk):
            for t in range(nt):
                w, scale = tile(w_x, (side,), t, k), tile(s_x, (side,), t, k)
                edge_side = LOW if t == 0 else HIGH if t == nt - 1 else None
                for c in range(3):
                    total = tile(acc_x, (side, c), t, k) + w * x_halo(side, c, t, k)
                    if edge_side is not None:
                        y_row = 0 if t == 0 else ROWS - 1
                        total = total + tile(w_xy, (side,), t, k) * moved(y_halo(edge_side, c, k), x, y_row)
                    value = (1.0 - RELAX) * tile(u, (c, x), t, k) + scale * total
                    if side == LOW:
                        put((x_low0, x_low1)[t], (c,), 0, k, value)
                    else:
                        put(x_high, (c,), t, k, value)


def energy_kernel(
    u_in, x_low0, x_low1, y_low, x_high, y_high, material, history_old, tough_from, damage_from, far_one, *rest
):
    *fars, u, u_out, history, top, half_top, far, half_far, tough, damage, rows, half_rows, sems = rest
    _, nx, ny, nz = u.shape
    nt, nk = ny // ROWS, nz // LANES
    x_low = (x_low0, x_low1)
    insert_faces(
        u,
        lambda side, c, t, k: x_part((x_low, x_high)[side], c, t, k),
        lambda side, c, k: tile((y_low, y_high)[side], (c,), 0, k),
    )
    me, size = lax.axis_index("yz"), lax.axis_size("yz")
    first, others = routes(size)
    sources = {0: tough_from.at[me], first: far_one.at[0]}
    for d, arrived in zip(others, fars):
        sources.update({d: arrived.at[0], d ^ 1: arrived.at[1]})
    copies = [pltpu.make_async_copy(u.at[c], u_out.at[c], sems.at[c]) for c in range(3)]
    copies += [pltpu.make_async_copy(source, tough.at[d], sems.at[4 + d]) for d, source in sources.items()]
    copies.append(pltpu.make_async_copy(damage_from, damage, sems.at[3]))
    start_all(copies)

    def body(x, place):
        lane, row = lane_index(), row_index()
        lines = {(c, t): Line(lambda k, c=c, t=t: tile(u, (c, x), t, k), nk) for c in range(3) for t in range(nt)}
        for k in range(nk):
            sums = [None] * nt
            for c in range(3):
                column = [lines[c, t].own(k) for t in range(nt)]
                ya = y_after(column)
                for t in range(nt):
                    v = column[t]
                    b = ya[t] - v
                    if t == nt - 1:
                        b = jnp.where(row == ROWS - 1, 0.0, b)
                    after = lines[c, t].after(k)
                    if k == nk - 1:
                        after = jnp.where(lane == LANES - 1, 0.0, after)
                    d = after - v
                    total = b * b + d * d
                    if place != 1:
                        a = tile(u, (c, x + 1), t, k) - v
                        total = total + a * a
                    sums[t] = total if c == 0 else sums[t] + total
            for t in range(nt):
                half = 0.5 * modulus(tile(material, (x,), t, k))
                if t == nt - 1:
                    put(rows, (x,), 0, k, sums[t])
                    put(half_rows, (x,), 0, k, half)
                if place == 1:
                    put(far, (), t, k, sums[t])
                    put(half_far, (), t, k, half)
                put(history, (x,), t, k, jnp.maximum(tile(history_old, (x,), t, k), half * sums[t]))

    planes_of(nx, body)
    for x in range(nx):
        top[x : x + 1, :] = rows[x, ROWS - 1 : ROWS, :]
        half_top[x : x + 1, :] = half_rows[x, ROWS - 1 : ROWS, :]
    for copy in copies:
        copy.wait()


def history_kernel(
    history_in, top, half_top, far, half_far, x_high, y_high, hy, hx0, hx1, history, energy
):
    nx, ny, nz = history.shape
    nt, nk = ny // ROWS, nz // LANES
    hx = (hx0, hx1)

    def squares(here, beyond):
        return sum([(beyond(c) - here(c)) ** 2 for c in range(3)])

    for k in range(nk):
        total = tile(top, (), 0, k) + squares(lambda c: tile(y_high, (c,), 0, k), lambda c: tile(hy, (c,), 0, k))
        put(energy, (), 0, k, tile(half_top, (), 0, k) * total)

    def body(x, _):
        for k in range(nk):
            value = jnp.where(row_index() == ROWS - 1, moved(tile(energy, (), 0, k), x, ROWS - 1), 0.0)
            put(history, (x,), nt - 1, k, jnp.maximum(tile(history, (x,), nt - 1, k), value))
        return 0

    lax.fori_loop(0, nx - 1, body, 0)
    for k in range(nk):
        y_term = squares(lambda c: tile(y_high, (c,), 0, k), lambda c: tile(hy, (c,), 0, k))
        for t in range(nt):
            total = tile(far, (), t, k) + squares(lambda c: tile(x_high, (c,), t, k), lambda c: x_part(hx, c, t, k))
            if t == nt - 1:
                total = total + jnp.where(row_index() == ROWS - 1, moved(y_term, nx - 1, ROWS - 1), 0.0)
            put(history, (nx - 1,), t, k, jnp.maximum(tile(history, (nx - 1,), t, k), tile(half_far, (), t, k) * total))


def last_kernel(ids, owners, history, damage, tough, hop_two, history_out, damage_out, result, sems):
    nx, ny, nz = damage.shape
    nt = ny // ROWS
    count = ids.shape[1]
    me, size = lax.axis_index("yz"), lax.axis_size("yz")
    late = routes(size)[0] ^ 1
    saved = pltpu.make_async_copy(history, history_out, sems.at[0])
    saved.start()
    rest = pltpu.make_async_copy(damage, damage_out, sems.at[1])
    rest.start()
    finished = []
    per = max(n for n in (1, 2, 3, 4, 6) if count % n == 0)
    cells = [(x, t) for x in range(nx) for t in range(nt)]
    i = lax.broadcasted_iota(jnp.int32, (2 * LANES, LANES), 0) % LANES
    j = lax.broadcasted_iota(jnp.int32, (2 * LANES, LANES), 1)
    beside = (i - j == 1) | (j - i == 1) | ((i == j) & ((i == 0) | (i == LANES - 1)))
    beside = jnp.where(beside, 1.0, 0.0).astype(jnp.bfloat16)

    def z_sums(d):
        whole = jnp.concatenate([d[cell] for cell in cells], axis=0)
        main = whole.astype(jnp.bfloat16)
        rest = (whole - main.astype(F32)).astype(jnp.bfloat16)
        sums = jnp.dot(jnp.concatenate([main, rest], axis=1), beside, preferred_element_type=F32)
        return {cell: sums[n * ROWS : (n + 1) * ROWS] for n, cell in enumerate(cells)}

    def sweep(first, second, d):
        row = row_index()
        sums, new = z_sums(d), {}
        for x in range(nx):
            column = [d[x, t] for t in range(nt)]
            yb, ya = y_before(column), y_after(column)
            yb[0] = jnp.where(row == 0, column[0], yb[0])
            ya[-1] = jnp.where(row == ROWS - 1, column[-1], ya[-1])
            for t in range(nt):
                total = (d[min(x + 1, nx - 1), t] + d[max(x - 1, 0), t]) + (ya[t] + yb[t]) + sums[x, t]
                new[x, t] = first[x, t] + second[x, t] * total
        return new

    def group(q):
        states = []
        for p in range(per):
            n = q * per + p
            owner = owners[0, n]
            slot = sum([(owners[0, m] == owner).astype(jnp.int32) for m in range(n)], jnp.int32(0))
            lanes = pl.ds(pl.multiple_of(ids[0, n] * LANES, LANES), LANES)
            which = (owner ^ me == late).astype(jnp.int32)
            by_hop = (owner ^ me == 1) | (owner ^ me == late)
            first, second, d = {}, {}, {}
            for x, t in cells:
                part = slice(t * ROWS, (t + 1) * ROWS)
                h2 = 2.0 * history[x, part, lanes]
                g = tough[owner ^ me, slot, x, part, :]
                g = jnp.where(by_hop, hop_two[which, slot, x, part, :], g)
                g2 = g * LENGTH
                inverse = 1.0 / (g / LENGTH + h2 + 6.0 * g2)
                first[x, t] = h2 * inverse
                second[x, t] = g2 * inverse
                d[x, t] = damage[x, part, lanes]
            states.append((n, lanes, first, second, d))
        for _ in range(SWEEPS):
            states = [(n, lanes, first, second, sweep(first, second, d)) for n, lanes, first, second, d in states]
        if q == 0:
            rest.wait()
        for n, lanes, _, _, d in states:
            for x, t in cells:
                part = slice(t * ROWS, (t + 1) * ROWS)
                result[n, x, part, :] = jnp.maximum(d[x, t], damage[x, part, lanes])
            finished.append(pltpu.make_async_copy(result.at[n], damage_out.at[:, :, lanes], sems.at[2 + n]))
            finished[-1].start()

    for q in range(count // per):
        group(q)
    for copy in [saved] + finished:
        copy.wait()


def even_pairs(axis):
    size = lax.axis_size(axis)
    pairs = [(i, i + 1) for i in range(0, size - 1, 2)]
    return pairs + [(b, a) for a, b in pairs]


def odd_pairs(axis):
    gx, yz = lax.axis_size("gx"), lax.axis_size("yz")

    def number(place, other):
        return place * yz + other if axis == "gx" else other * yz + place

    size, others = (gx, yz) if axis == "gx" else (yz, gx)
    step = 2 if axis == "gx" else 1
    pairs = [(number(i, o), number(i + 1, o)) for i in range(1, size - 1, 2) for o in range(others)]
    if size % 2 == 0 and others % (2 * step) == 0:
        for end in (0, size - 1):
            pairs += [(number(end, o), number(end, o + step)) for o in range(others) if o % (2 * step) < step]
    return pairs + [(b, a) for a, b in pairs]


def exchange(ye, yo, xe0, xe1, xo0, xo1):
    both = ("gx", "yz")
    return (
        lax.ppermute(xe0, "gx", even_pairs("gx")),
        lax.ppermute(ye, "yz", even_pairs("yz")),
        lax.ppermute(yo, both, odd_pairs("yz")),
        lax.ppermute(xe1, "gx", even_pairs("gx")),
        lax.ppermute(xo0, both, odd_pairs("gx")),
        lax.ppermute(xo1, both, odd_pairs("gx")),
    )


def routes(size):
    assert size >= 8 and size & (size - 1) == 0
    return 4, tuple(d for d in (6, 2) + tuple(range(8, size, 2)))


def across(value, d):
    return lax.ppermute(value, "yz", [(i, i ^ d) for i in range(lax.axis_size("yz"))])


def from_above(value, axis):
    size = lax.axis_size(axis)
    return lax.ppermute(value, axis, [(i + 1, i) for i in range(size - 1)])


def call(kernel, outs, ins, scratch=(), aliases=None):
    args, in_specs, out_specs, shapes = [], [], [], []
    for value, space in ins:
        args.append(value if space is pltpu.SMEM else pltpu.with_memory_space_constraint(value, space))
        in_specs.append(pl.BlockSpec(memory_space=space))
    for shape, space in outs:
        shapes.append(space(shape, F32))
        out_specs.append(pl.BlockSpec(memory_space=space))
    return pl.pallas_call(
        kernel,
        out_shape=shapes,
        in_specs=in_specs,
        out_specs=out_specs,
        scratch_shapes=scratch,
        input_output_aliases=aliases or {},
        compiler_params=pltpu.CompilerParams(vmem_limit_bytes=GRANT),
    )(*args)


def here(*shapes):
    return [(shape, VMEM) for shape in shapes]


def kept(*values):
    return [(value, VMEM) for value in values]


def far_off(*values):
    return [(value, HBM) for value in values]


def body(displacement, force, damage, history_old, material, patch_ids, owners, toughness):
    nx, ny, nz = damage.shape
    assert nx == ROWS and ny == 2 * ROWS
    full, cells, halves = (3, nx, ny, nz), (nx, ny, nz), (3, ROWS, nz)

    def faces(count, extra):
        return here(*[(count, nx, nz)] * 2, *[(count, ROWS, nz)] * 2, *[(count, ROWS, nz + extra)] * 2)

    def copies(count):
        return pltpu.SemaphoreType.DMA((count,))

    tough = toughness[0]
    pair = (2,) + tough.shape[1:]
    first, others = routes(lax.axis_size("yz"))
    u, stiff, *sent, far_one = call(
        begin_kernel,
        here(full, cells) + faces(4, LANES) + here(pair),
        far_off(damage, material, displacement, tough),
        [pltpu.VMEM(cells, F32), pltpu.VMEM(cells, jnp.int32), pltpu.SemaphoreType.DMA((4, nx))],
    )
    brought = exchange(*sent)
    far_one = across(far_one, first)
    wx, wya, wyb, wza, wzb, scale, u1, acc_x, acc_y, diag_x, diag_y, hop = call(
        inner_one_kernel,
        here((nx - 1, ny, nz), *[cells] * 5, full, (2, 3, ny, nz), (2, 3, nx, nz), (2, ny, nz), (2, 1, nx, nz))
        + here((len(others),) + tough.shape[1:]),
        kept(u, stiff, force) + far_off(tough) + kept(brought[0], brought[3]),
        [pltpu.VMEM((2, 3, nx, ROWS, nz), F32), pltpu.VMEM((2, 1, nx, ROWS, nz), F32), copies(len(others))],
    )
    *own, w_x, w_xy, s_x, w_y, w_yx, s_y, planes, hop = call(
        face_one_kernel,
        faces(3, 0) + here(*[(2, ny, nz)] * 3, *[(2, nx, nz)] * 3, (2, 3, ny, nz), hop.shape),
        kept(u, stiff, sent[0], sent[1], acc_x, acc_y, diag_x, diag_y, *brought, hop),
        (),
        {14: 13},
    )
    hop = across(hop, 1)
    brought = exchange(*own)
    u1, u2, acc_x, acc_y, hop_two, *fars = call(
        inner_two_kernel,
        here(full, full, (2, 3, ny, nz), (2, 3, nx, nz), pair, *[pair for _ in others]),
        kept(u1, scale, force, wx, wya, wyb, wza, wzb, own[0], own[1], planes)
        + far_off(tough)
        + kept(far_one, brought[0], brought[3]),
        [pltpu.VMEM((2, 3, nx, ROWS, nz), F32), copies(2 + len(others))],
        {0: 0},
    )
    fars = call(forward_kernel, here(*[pair for _ in others]), kept(hop, *fars), (), {1 + i: i for i in range(len(others))})
    lasts = [across(value, d) for d, value in zip(others, fars)]
    x_low0, x_low1, y_low, x_high, y_high, hop_two = call(
        face_two_kernel,
        here(halves, halves, (3, nx, nz + LANES), (3, ny, nz), (3, nx, nz), hop_two.shape),
        kept(u1, own[0], own[1], acc_x, acc_y, w_x, w_xy, s_x, w_y, w_yx, s_y, *brought, hop_two),
        (),
        {17: 5},
    )
    hop_two = across(hop_two, 1)
    hy, hx0, hx1 = from_above(y_low, "yz"), from_above(x_low0, "gx"), from_above(x_low1, "gx")
    _, new_displacement, history, *sums, tough_kept, damage_kept = call(
        energy_kernel,
        here(full) + [(full, HBM)] + here(cells, *[(nx, nz)] * 2, *[(ny, nz)] * 2, tough.shape, cells),
        kept(u2, x_low0, x_low1, y_low, x_high, y_high, material, history_old) + far_off(tough, damage)
        + kept(far_one, *lasts),
        [pltpu.VMEM((nx, ROWS, nz), F32), pltpu.VMEM((nx, ROWS, nz), F32), copies(4 + tough.shape[0])],
        {0: 0},
    )
    (history,) = call(
        history_kernel,
        here(cells),
        kept(history, *sums, x_high, y_high, hy, hx0, hx1),
        [pltpu.VMEM((nx, nz), F32)],
        {0: 0},
    )
    count = patch_ids.shape[1]
    new_history, new_damage = call(
        last_kernel,
        [(cells, HBM), (cells, HBM)],
        [(patch_ids, pltpu.SMEM), (owners[:, :, 0], pltpu.SMEM)] + kept(history, damage_kept, tough_kept, hop_two),
        [pltpu.VMEM((count, nx, ny, LANES), F32), copies(2 + count)],
    )
    return (new_displacement, new_history, new_damage)


def solution(mesh):
    return jax.shard_map(
        body,
        mesh=mesh,
        in_specs=(
            P(None, "gx", "yz", None),
            P(None, "gx", "yz", None),
            P("gx", "yz", None),
            P("gx", "yz", None),
            P("gx", "yz", None),
            P(("gx", "yz"), None),
            P(("gx", "yz"), None, None),
            P(("gx", "yz"), None, None, None, None, None),
        ),
        out_specs=(P(None, "gx", "yz", None), P("gx", "yz", None), P("gx", "yz", None)),
        check_vma=False,
    )
```
